256 devices in a mesh: gx: 4 (over x), gy: 4 (over y), gz: 16 (over z, core).
Axes of the slice: x: 4, y: 4, z: 8, core: 2. Of those that a mesh axis runs over, the one named last changes fastest.
Arguments:
- leaf_offsets: float32 [3, 524288], P(None, ('gx', 'gy', 'gz')), may hold values from -0.5 to 0.5
- latent_charges: float32 [524288], P(('gx', 'gy', 'gz')), may hold values from -0.2 to 0.2
- atom_counts: int32 [8192], P(('gx', 'gy', 'gz')), may hold values from 1 to 64
- near_boxes: int32 [26, 8192], P(None, ('gx', 'gy', 'gz')), may hold values from -1 to 8191, as said below
- far_slots: int32 [189, 8192], P(None, ('gx', 'gy', 'gz')), may hold values from -1 to 95, as said below
- branch_slots: int32 [256, 8, 8], P(('gx', 'gy', 'gz')), may hold values from 0 to 87, as said below
- far_operators: bfloat16 [165, 31185], replicated, may hold values from -0.5 to 0.5
Outputs:
- potential: float32 [524288], P(('gx', 'gy', 'gz'))
The draws below stay inside these ranges and needn't reach their ends.
Inputs may be any that keep to these rules, and one draw needn't show every extreme that they name: `near_boxes`: an entry names a box owned by the same device as box g or by its neighbour one step along gz (never past the ends of gz), lying within 8 boxes of the device's own range; or it is -1. `far_slots`: an entry is -1 or a slot of the held set of the device that owns box g. branch_slots[d, k, j] is below 32 + k * 8: a slot that device d holds before section k.
All inputs are finite; a program needn't handle non-finite values.
Results may differ from the reference program's by a relative error of at most 0.0017.
Values may be sent and summed in bfloat16 or wider, within the bound.
A program may use at most 128 MiB of HBM per device.

```python
import math
import jax
import jax.numpy as jnp
import numpy as np
from jax import lax

ORDER = 8
SLOTS = 64
NEAR = 26
LIST = 189
BOX_DEV = 32
TERMS = 165
SEND = 8
HALO = 8
LOGD = 8
CAP = 96
BOXES = 8192
ATOMS = 524288
N_GZ = 16
DEVICES = 256


def draw_near_boxes(key, part):
    key = jax.random.fold_in(key, 11)
    key_pick, key_keep = jax.random.split(key)
    owner_dev = jnp.arange(BOXES, dtype=jnp.int32) // BOX_DEV
    gz_place = owner_dev % N_GZ
    low_bound = jnp.where(gz_place > 0, owner_dev * BOX_DEV - HALO, owner_dev * BOX_DEV)
    high_bound = jnp.where(gz_place < N_GZ - 1, (owner_dev + 1) * BOX_DEV + HALO, (owner_dev + 1) * BOX_DEV)
    raw_draw = jax.random.randint(key_pick, (NEAR, BOXES), 0, 1 << 20, dtype=jnp.int32)
    chosen = raw_draw % (high_bound - low_bound)[None, :] + low_bound[None, :]
    retain = jax.random.randint(key_keep, (NEAR, BOXES), 0, 8, dtype=jnp.int32) < 7
    boxes_out = jnp.where(retain, chosen, -1)
    position = jnp.arange(BOXES, dtype=jnp.int32) % BOX_DEV
    boxes_out = boxes_out.at[0].set(jnp.where(position == BOX_DEV - 1, high_bound - 1, boxes_out[0]))
    boxes_out = boxes_out.at[NEAR - 1].set(jnp.where(position == 0, -1, boxes_out[NEAR - 1]))
    return boxes_out.astype(jnp.int32)


def draw_far_slots(key, part):
    key = jax.random.fold_in(key, 23)
    key_pick, key_keep = jax.random.split(key)
    chosen = jax.random.randint(key_pick, (LIST, BOXES), 0, CAP, dtype=jnp.int32)
    retain = jax.random.randint(key_keep, (LIST, BOXES), 0, 8, dtype=jnp.int32) < 7
    slots_out = jnp.where(retain, chosen, -1)
    position = jnp.arange(BOXES, dtype=jnp.int32) % BOX_DEV
    slots_out = slots_out.at[0].set(jnp.where(position == BOX_DEV - 1, CAP - 1, slots_out[0]))
    slots_out = slots_out.at[LIST - 1].set(jnp.where(position == 0, -1, slots_out[LIST - 1]))
    return slots_out.astype(jnp.int32)


def draw_branch_slots(key, part):
    key = jax.random.fold_in(key, 37)
    limits = BOX_DEV + SEND * jnp.arange(LOGD, dtype=jnp.int32)
    raw_draw = jax.random.randint(key, (DEVICES, LOGD, SEND), 0, 1 << 20, dtype=jnp.int32)
    slots_out = raw_draw % limits[None, :, None]
    slots_out = slots_out.at[:, LOGD - 1, SEND - 1].set(BOX_DEV + (LOGD - 1) * SEND - 1)
    slots_out = slots_out.at[:, 0, 0].set(0)
    return slots_out.astype(jnp.int32)


def set_ends(drawn, stream_key, low, largest):
    longest = drawn.shape.index(max(drawn.shape))
    spots = []
    for shift in (0, 1):
        where = [jax.random.randint(jax.random.fold_in(stream_key, axis), (), 0, length) for axis, length in enumerate(drawn.shape)]
        where[longest] = (where[longest] + shift) % drawn.shape[longest]
        spots.append(tuple(where))
    return drawn.at[spots[0]].set(low).at[spots[1]].set(largest)


def steps_of(key, extent, pieces, least, high):
    def one(axis_at, shards_of):
        heights = jax.random.uniform(jax.random.fold_in(jax.random.fold_in(key, 6), axis_at), (shards_of,), jnp.float32, least / len(pieces), high / len(pieces))
        return jnp.repeat(jnp.exp(heights), extent[axis_at] // shards_of).reshape((-1,) + (1,) * (len(extent) - axis_at - 1))

    level = one(*pieces[0])
    for cut in pieces[1:]:
        level = level * one(*cut)
    return level


def noise(rng, dims, scale, reach, cuts=(), held_as=jnp.bfloat16):
    entries = scale * jax.random.normal(rng, dims, jnp.float32)
    if cuts:
        entries = entries * steps_of(rng, dims, cuts, -0.22, 0.18)
    return jnp.clip(entries, -reach, reach).astype(held_as)


def setup_inputs(seed: int = 0) -> dict:
    streams_of = jax.random.split(jax.random.key(seed), 8)
    return {
        "leaf_offsets": jnp.clip(jax.random.uniform(streams_of[0], (3, ATOMS), jnp.float32, -0.5, 0.5) * steps_of(streams_of[0], (3, ATOMS), ((1, 256),), -0.4, 0.0), -0.5, 0.5),
        "latent_charges": noise(streams_of[1], (ATOMS,), 0.03, 0.2, ((0, 256),), jnp.float32),
        "atom_counts": set_ends(jax.random.randint(streams_of[2], (BOXES,), 1, SLOTS + 1), jax.random.fold_in(streams_of[2], 1), 1, SLOTS).astype(jnp.int32),
        "near_boxes": draw_near_boxes(jax.random.fold_in(streams_of[7], 71), 0),
        "far_slots": draw_far_slots(jax.random.fold_in(streams_of[7], 71), 0),
        "branch_slots": draw_branch_slots(jax.random.fold_in(streams_of[7], 71), 0),
        "far_operators": noise(streams_of[6], (TERMS, LIST * TERMS), TERMS ** -0.5, 0.5),
    }


soften = 0.25

def term_table():
    listed = [(first_exp, second_exp, degree - first_exp - second_exp) for degree in range(ORDER + 1) for first_exp in range(degree, -1, -1) for second_exp in range(degree - first_exp, -1, -1)]
    return np.array(listed, dtype=np.int32)

def monomials(scaled):
    table_np = term_table()
    stacked = [jnp.ones_like(scaled)]
    for degree in range(ORDER):
        stacked.append(stacked[-1] * scaled)
    powers = jnp.stack(stacked, 0)
    return powers[table_np[:, 0], 0] * powers[table_np[:, 1], 1] * powers[table_np[:, 2], 2]

def shift_table():
    listed = [(first_step, second_step, third_step) for first_step in (-1, 0, 1) for second_step in (-1, 0, 1) for third_step in (-1, 0, 1) if first_step != 0 or second_step != 0 or third_step != 0]
    return np.array(listed, dtype=np.float32).T

def near_block(target, source_pos, source_q, shifts):
    dist_sq = soften * soften
    for axis_num in range(3):
        spacing = shifts[axis_num][:, None, None, None] + source_pos[axis_num][:, :, None, :] - target[axis_num][None, :, :, None]
        dist_sq = dist_sq + spacing * spacing
    return lax.optimization_barrier(jnp.sum(source_q[:, :, None, :] * lax.rsqrt(dist_sq), axis=(0, 3)))

def self_block(target, target_q):
    dist_sq = soften * soften
    for axis_num in range(3):
        spacing = target[axis_num][:, None, :] - target[axis_num][:, :, None]
        dist_sq = dist_sq + spacing * spacing
    slot_count = target.shape[-1]
    distinct = jnp.arange(slot_count)[:, None] != jnp.arange(slot_count)[None, :]
    return lax.optimization_barrier(jnp.sum(jnp.where(distinct[None], target_q[:, None, :] * lax.rsqrt(dist_sq), 0.0), axis=2))

def near_field(positions, masked, near_boxes):
    shifts = shift_table()
    block_len = math.gcd(BOXES, 16)

    def one_block(block_id):
        first_box = block_id * block_len
        target = lax.dynamic_slice_in_dim(positions, first_box, block_len, 1)
        target_q = lax.dynamic_slice_in_dim(masked, first_box, block_len, 0)
        sources = lax.dynamic_slice_in_dim(near_boxes, first_box, block_len, 1)
        present = sources >= 0
        clipped = jnp.clip(sources, 0, BOXES - 1)
        source_pos = positions[:, clipped]
        source_q = jnp.where(present[:, :, None], masked[clipped], 0.0)
        return self_block(target, target_q) + near_block(target, source_pos, source_q, shifts)
    return lax.map(one_block, jnp.arange(BOXES // block_len, dtype=jnp.int32)).reshape(BOXES, SLOTS)

def reference(leaf_offsets, latent_charges, atom_counts, near_boxes, far_slots, branch_slots, far_operators):
    filled = jnp.arange(SLOTS, dtype=jnp.int32)[None, :] < atom_counts[:, None]
    masked = jnp.where(filled, latent_charges.reshape(BOXES, SLOTS), 0.0)
    positions = leaf_offsets.reshape(3, BOXES, SLOTS)
    term_values = monomials(2.0 * leaf_offsets).reshape(TERMS, BOXES, SLOTS)
    multipoles = jnp.einsum('kbs,bs->kb', term_values, masked, precision=lax.Precision.HIGHEST).astype(jnp.bfloat16)
    held_terms = multipoles.reshape(TERMS, DEVICES, BOX_DEV).transpose(1, 0, 2)
    devices_all = jnp.arange(DEVICES, dtype=jnp.int32)
    for section_idx in range(LOGD):
        chosen = branch_slots[:, section_idx, :]
        payload = jnp.take_along_axis(held_terms, chosen[:, None, :], axis=2)
        partner = jnp.bitwise_xor(devices_all, 1 << section_idx)
        held_terms = jnp.concatenate([held_terms, payload[partner]], axis=2)
    flat_held = held_terms.transpose(1, 0, 2).reshape(TERMS, DEVICES * CAP)
    owner_dev = jnp.arange(BOXES, dtype=jnp.int32) // BOX_DEV
    operators = far_operators.reshape(TERMS, LIST, TERMS).transpose(1, 0, 2)

    def add_term(local_terms, inputs):
        operator, slots_row = inputs
        columns = flat_held[:, owner_dev * CAP + jnp.clip(slots_row, 0, CAP - 1)]
        columns = jnp.where(slots_row[None, :] >= 0, columns, jnp.zeros((), jnp.bfloat16))
        return (local_terms + jnp.dot(operator, columns, preferred_element_type=jnp.float32), None)
    local_terms = lax.scan(add_term, jnp.zeros((TERMS, BOXES), jnp.float32), (operators, far_slots))[0]
    far_field_sum = jnp.einsum('kb,kbs->bs', local_terms, term_values, precision=lax.Precision.HIGHEST)
    near_field_sum = near_field(positions, masked, near_boxes)
    potential = jnp.where(filled, near_field_sum + far_field_sum, 0.0)
    return potential.reshape(ATOMS)
```

```python
import itertools

import jax
import jax.numpy as jnp
import numpy as np
from jax import lax
from jax.experimental import pallas as pl
from jax.experimental.pallas import tpu as pltpu
from jax.sharding import PartitionSpec as P

ORDER = 8
TERMS = 165
ROWS = 168
LIST = 189
BOXES = 32
SLOTS = 64
ATOMS = BOXES * SLOTS
HALO = 8
EXT = BOXES + 2 * HALO
SOFT2 = 0.0625
GROUP = 16
F32 = jnp.float32
BF16 = jnp.bfloat16
NT = (((1,), (1,)), ((), ()))
MESH = pl.DeviceIdType.MESH
SHIFTS = [s for s in itertools.product((-1, 0, 1), repeat=3) if s != (0, 0, 0)] + [(0, 0, 0)] * 2
PAIRS = len(SHIFTS) // 2


def degree_start(n):
    return n * (n + 1) * (n + 2) // 6


def low(m):
    return (m & -m).bit_length() - 1


def flipped(v, mask, bits):
    for b in range(bits):
        if mask >> b & 1:
            v = v + (1 << b) - (2 << b) * ((v // (1 << b)) % 2)
    return v


def partner(rnd, m):
    if rnd == 0:
        return {"gz": flipped(lax.axis_index("gz"), m, 4)}
    return {
        "gy": flipped(lax.axis_index("gy"), m & 3, 2),
        "gx": flipped(lax.axis_index("gx"), m >> 2, 2),
    }


def iota(shape, dim):
    return lax.broadcasted_iota(jnp.int32, shape, dim)


def fiota(shape, dim):
    return iota(shape, dim).astype(F32)


def split2(v):
    hi = v.astype(BF16)
    return hi, (v - hi.astype(F32)).astype(BF16)


def split3(v):
    hi = v.astype(BF16)
    rest = v - hi.astype(F32)
    mid = rest.astype(BF16)
    return hi, mid, (rest - mid.astype(F32)).astype(BF16)


def dot(a, b, dims=None):
    if dims is None:
        return jnp.dot(a, b, preferred_element_type=F32)
    return lax.dot_general(a, b, dims, preferred_element_type=F32)


def onehot(cond):
    return jnp.where(cond, 1.0, 0.0)


def main_tail_rows(cols, step, width):
    lanes = fiota((8, width), 1)
    rows = []
    for i in range(4):
        at = cols[8 * i : 8 * i + 8]
        rows.append(onehot(lanes == at))
        rows.append(onehot(lanes == at + step))
    return jnp.concatenate(rows, axis=0).astype(BF16)


def routed(tab_rows, tab_cols, base):
    lane = fiota((1, 128), 1)
    lane8 = (iota((1, 128), 1) % 8).astype(F32)
    sub = fiota((32, 1), 0)
    sub8 = (iota((32, 1), 0) % 8).astype(F32)

    def first_row(m):
        s = tab_rows[m : m + 1]
        return jnp.where(s < base, 16.0 * (m - 1) + lane8, 16.0 * m + s - base)

    def first_col(m):
        s = tab_cols[:32, m : m + 1]
        return jnp.where(s < base, 16.0 * (m - 1) + sub8, 16.0 * m + s - base)

    def looked_up(m, table_row, section):
        s = tab_cols[8 * section : 8 * section + 8, m : m + 1]
        lanes = fiota((8, 128), 1)
        found = jnp.sum(jnp.where(lanes == s - base, table_row, 0.0), axis=1, keepdims=True)
        return jnp.where(s < base, 16.0 * (m - 1) + sub8[:8], found)

    table4 = jnp.where(lane < 8, 16.0 * 4 + lane8, first_row(6))
    table12 = jnp.where(sub < 8, 16.0 * 12 + sub8, first_col(14))
    s12 = tab_rows[12:13]
    found12 = jnp.sum(jnp.where(fiota((32, 128), 0) == s12 - base, table12, 0.0), axis=0, keepdims=True)
    row12 = jnp.where(s12 < base, 16.0 * 11 + lane8, found12)
    table8 = jnp.where(lane < 8, 16.0 * 8 + lane8, jnp.where(lane < 16, first_row(10), row12))
    return jnp.concatenate(
        [sub8[:8], first_col(2)[8:16], looked_up(4, table4, 2), looked_up(8, table8, 3)], axis=0
    )


def kernel(
    offs_ref, q_ref, counts_ref, near_ref, far_ref, branch_ref, op_hbm, shift_ref, out_ref,
    opv, tv, p8, dup, tcol, accs, tabrow, tabs, own2, snd1, snd2, rcv1, rcv2, held, oh, col, tail,
    op_sem, tss, trs, hss, hrs, ss1, rs1, ss2, rs2,
):
    op_copy = pltpu.make_async_copy(op_hbm, opv, op_sem)
    op_copy.start()
    gz = lax.axis_index("gz")
    gzs = lax.axis_size("gz")
    barrier = pltpu.get_barrier_semaphore()
    for rnd in range(2):
        for m in range(1, GROUP):
            pl.semaphore_signal(barrier, inc=1, device_id=partner(rnd, m), device_id_type=MESH)

    lo8 = iota((8, 128), 1) < SLOTS
    slot_in_box = iota((1, 128), 1) % SLOTS
    lo1 = iota((1, 128), 1) < SLOTS
    p8[...] = jnp.zeros((8, ATOMS), F32)
    p8[0:3, :] = offs_ref[...]
    for r in range(BOXES // 2):
        count = jnp.where(lo1, counts_ref[2 * r], counts_ref[2 * r + 1])
        span = slice(128 * r, 128 * r + 128)
        p8[3:4, span] = jnp.where(slot_in_box < count, q_ref[:, span], 0.0)
    for r in range(BOXES // 2):
        span = slice(128 * r, 128 * r + 128)
        here = p8[:, span]
        other = pltpu.roll(here, SLOTS, 1)
        dup[HALO + 2 * r] = jnp.where(lo8, here, other)
        dup[HALO + 2 * r + 1] = jnp.where(lo8, other, here)
        tcol[span, :] = jnp.transpose(here)
    dup[EXT] = jnp.zeros((8, 128), F32)

    branch = branch_ref[0].astype(F32).astype(BF16)
    spread = onehot(iota((8, 128), 1) % 8 == iota((8, 128), 0)).astype(BF16)
    wide = dot(branch, spread)
    tabrow[...] = jnp.sum(
        jnp.where(iota((8, 128), 1) // 8 == iota((8, 128), 0), wide, 0.0), axis=0, keepdims=True
    )
    stretch = onehot(iota((64, 8), 0) // 8 == iota((64, 8), 1)).astype(BF16)
    tall = dot(stretch, branch)
    scol = jnp.sum(jnp.where(iota((64, 8), 1) == iota((64, 8), 0) % 8, tall, 0.0), axis=1, keepdims=True)

    def terms_block(blk, _):
        span = pl.ds(pl.multiple_of(blk * 256, 256), 256)
        x, y, z = (2.0 * p8[c : c + 1, span] for c in range(3))
        tv[0:1, span] = jnp.ones((1, 256), F32)
        for n in range(1, ORDER + 1):
            before, here, kept = degree_start(n - 1), degree_start(n), n * (n + 1) // 2
            tv[here : here + kept, span] = tv[before : before + kept, span] * x
            tv[here + kept : here + kept + n, span] = tv[before + kept - n : before + kept, span] * y
            tv[here + kept + n : here + kept + n + 1, span] = tv[before + kept - 1 : before + kept, span] * z
        tv[TERMS:ROWS, span] = jnp.zeros((ROWS - TERMS, 256), F32)
        return 0

    lax.fori_loop(0, ATOMS // 256, terms_block, 0)

    pl.semaphore_wait(barrier, 2 * (GROUP - 1))
    sends = []
    table_copies = []
    for rnd in range(2):
        for m in range(1, GROUP):
            at = rnd * GROUP + m
            c = pltpu.make_async_remote_copy(
                src_ref=tabrow, dst_ref=tabs.at[at], send_sem=tss.at[at], recv_sem=trs.at[at],
                device_id=partner(rnd, m), device_id_type=MESH,
            )
            c.start()
            table_copies.append(c)
    up = pltpu.make_async_remote_copy(
        src_ref=dup.at[pl.ds(BOXES, HALO)], dst_ref=dup.at[pl.ds(0, HALO)],
        send_sem=hss.at[0], recv_sem=hrs.at[0], device_id={"gz": (gz + 1) % gzs}, device_id_type=MESH,
    )
    down = pltpu.make_async_remote_copy(
        src_ref=dup.at[pl.ds(HALO, HALO)], dst_ref=dup.at[pl.ds(BOXES + HALO, HALO)],
        send_sem=hss.at[1], recv_sem=hrs.at[1], device_id={"gz": (gz + gzs - 1) % gzs}, device_id_type=MESH,
    )
    up.start()
    down.start()

    head = jnp.zeros((64, ROWS), F32)
    rest = jnp.zeros((32, ROWS), F32)
    for blk in range(ATOMS // 256):
        span = slice(256 * blk, 256 * blk + 256)
        mine = (256 * blk + iota((BOXES, 256), 1)) // SLOTS == iota((BOXES, 256), 0)
        qh, qm = split2(jnp.where(mine, p8[3:4, span], 0.0))
        th, tm = split2(tv[:, span])
        head = head + dot(jnp.concatenate([qh, qm], axis=0), th, NT)
        rest = rest + dot(qh, tm, NT)
    multipoles = head[:32] + head[32:] + rest
    tail[...] = jnp.zeros((32, 128), F32)
    tail[:, 0 : ROWS - 128] = multipoles[:, 128:ROWS]
    own_main = multipoles[:, 0:128].astype(BF16)
    own_tail = tail[...].astype(BF16)
    own2[0:32] = own_main
    own2[32:64] = own_tail
    held[0:32, 0:128] = own_main
    held[0:32, 128:256] = own_tail

    picked1 = jnp.where(scol[:32] < 32, scol[:32], -1000.0)
    snd1[...] = dot(main_tail_rows(picked1, 32.0, 64), own2[...]).astype(BF16).reshape(4, 16, 128)

    def exchange(rnd, snd, rcv, ss, rs):
        out = []
        for m in range(1, GROUP):
            c = pltpu.make_async_remote_copy(
                src_ref=snd.at[low(m)], dst_ref=rcv.at[m - 1], send_sem=ss.at[m - 1], recv_sem=rs.at[m - 1],
                device_id=partner(rnd, m), device_id_type=MESH,
            )
            c.start()
            out.append(c)
        return out

    round1 = exchange(0, snd1, rcv1, ss1, rs1)

    for c in table_copies:
        c.wait_recv()
    tabs[0] = tabrow[...]
    tabs[GROUP] = tabrow[...]
    rows1 = jnp.concatenate([tabs[m] for m in range(GROUP)], axis=0)
    rows2 = jnp.concatenate([tabs[GROUP + m] for m in range(GROUP)], axis=0)
    cols1 = jnp.transpose(jnp.concatenate([rows1, rows2] + [jnp.zeros((96, 128), F32)], axis=0))
    from1 = routed(rows1, cols1[0:32, 0:16], 32.0)
    from2 = routed(pltpu.roll(rows2, 96, 1), cols1[32:64, 16:32], 64.0)
    own_late = scol[32:64]
    fwd = onehot(fiota((32, 32), 1) == own_late - 32.0).astype(BF16)
    via = dot(fwd, jnp.broadcast_to(from1, (32, 128)).astype(BF16))[:, 0:1]
    late = jnp.where(jnp.logical_and(own_late >= 32, own_late < 64), via, -1000.0)
    lanes240 = fiota((32, 240), 1)
    select1 = jnp.concatenate(
        [
            main_tail_rows(late, 8.0, 240),
            onehot(lanes240 == from1).astype(BF16),
            onehot(lanes240 == from1 + 8.0).astype(BF16),
        ],
        axis=0,
    )
    select2 = jnp.concatenate(
        [onehot(lanes240 == from2).astype(BF16), onehot(lanes240 == from2 + 8.0).astype(BF16)], axis=0
    )
    picked2 = jnp.where(own_late < 32, own_late, -1000.0)
    from_own = dot(main_tail_rows(picked2, 32.0, 64), own2[...])

    up.wait_recv()
    down.wait_recv()
    base_box = (
        (lax.axis_index("gx") * lax.axis_size("gy") + lax.axis_index("gy")) * gzs + gz
    ) * BOXES - HALO

    def near_box(g, _):
        lo = iota((8, 128), 1) < SLOTS
        at = pl.ds(pl.multiple_of(g * SLOTS, SLOTS), SLOTS)
        targets = tcol[at, :]
        t = [
            [jnp.broadcast_to(targets[8 * k : 8 * k + 8, c : c + 1], (8, 128)) for k in range(8)]
            for c in range(3)
        ]
        acc = [jnp.zeros((8, 128), F32) for _ in range(8)]
        for p in range(PAIRS):
            if p < PAIRS - 1:
                first, second = near_ref[2 * p, g], near_ref[2 * p + 1, g]
                first = jnp.where(first < 0, EXT, jnp.clip(first - base_box, 0, EXT - 1))
                second = jnp.where(second < 0, EXT, jnp.clip(second - base_box, 0, EXT - 1))
                src = jnp.where(lo, dup[first], dup[second]) + shift_ref[p]
            else:
                src = jnp.where(lo, dup[g + HALO], 0.0)
            sx, sy, sz, sq = (jnp.broadcast_to(src[c : c + 1], (8, 128)) for c in range(4))
            for k in range(8):
                dx, dy, dz = sx - t[0][k], sy - t[1][k], sz - t[2][k]
                weight = sq
                if p == PAIRS - 1:
                    weight = jnp.where(iota((8, 128), 1) == 8 * k + iota((8, 128), 0), 0.0, sq)
                acc[k] = acc[k] + weight * lax.rsqrt(dx * dx + (dy * dy + (dz * dz + SOFT2)))
        accs[at, :] = jnp.concatenate(acc, axis=0)
        return 0

    lax.fori_loop(0, BOXES // 2, near_box, 0)

    for c in round1:
        c.wait_recv()
    got = dot(select1, rcv1[...].reshape(240, 128))
    snd2[...] = (got[0:64] + from_own).astype(BF16).reshape(4, 16, 128)
    round2 = exchange(1, snd2, rcv2, ss2, rs2)
    held[32:64, 0:128] = got[64:96].astype(BF16)
    held[32:64, 128:256] = got[96:128].astype(BF16)

    far_cols = jnp.transpose(
        jnp.concatenate(
            [
                jnp.concatenate([far_ref[...].astype(F32), jnp.zeros((256 - LIST, BOXES), F32)], axis=0),
                jnp.zeros((256, 96), F32),
            ],
            axis=1,
        )
    )
    lanes96 = fiota((BOXES, 96), 1)
    for l in range(LIST):
        oh[BOXES * l : BOXES * l + BOXES, :] = onehot(lanes96 == far_cols[0:BOXES, l : l + 1]).astype(BF16)
    lax.fori_loop(BOXES // 2, BOXES, near_box, 0)
    ah, am = split2(accs[...])
    ones = jnp.ones((8, 128), BF16)
    near_row = (dot(ones, ah, NT) + dot(ones, am, NT))[0:1]

    for c in round2:
        c.wait_recv()
    got2 = dot(select2, rcv2[...].reshape(240, 128))
    held[64:96, 0:128] = got2[0:32].astype(BF16)
    held[64:96, 128:256] = got2[32:64].astype(BF16)

    table = held[...]

    lane32 = iota((BOXES, 128), 1)

    def gather(grp, carry):
        span = pl.ds(pl.multiple_of(grp * (7 * BOXES), 7 * BOXES), 7 * BOXES)
        seven = dot(oh[span, :], table)
        for i in range(7):
            pos = (grp * 7 + i) * TERMS
            r = pos % 128
            tile = pos // 128
            piece = seven[BOXES * i : BOXES * i + BOXES]
            a = pltpu.roll(piece[:, 0:128], r, 1)
            b = pltpu.roll(piece[:, 128:256], r, 1)
            before = lane32 < r
            one = jnp.where(before, carry, a)
            two = jnp.where(before, a, b)
            col[:, pl.ds(pl.multiple_of(tile * 128, 128), 128)] = one.astype(BF16)
            col[:, pl.ds(pl.multiple_of(tile * 128 + 128, 128), 128)] = two.astype(BF16)
            carry = jnp.where(r + TERMS >= 256, b, two)
        return carry

    last = lax.fori_loop(0, LIST // 7, gather, jnp.zeros((BOXES, 128), F32))
    op_copy.wait()
    local = dot(opv[...], col[:, 0 : LIST * TERMS], NT)

    l1, l2, l3 = split3(local)
    parts = jnp.concatenate([l1.astype(F32), l2.astype(F32), l3.astype(F32)], axis=1).astype(BF16)
    for blk in range(ATOMS // 256):
        span = slice(256 * blk, 256 * blk + 256)
        boxes = onehot((256 * blk + iota((96, 256), 1)) // SLOTS == iota((96, 256), 0) % BOXES).astype(BF16)
        there = dot(parts, boxes)
        far = jnp.sum(there * tv[0:TERMS, span], axis=0, keepdims=True)
        both = far + near_row[:, span]
        for h in range(2):
            r = 2 * blk + h
            count = jnp.where(lo1, counts_ref[2 * r], counts_ref[2 * r + 1])
            out_ref[:, 128 * r : 128 * r + 128] = jnp.where(
                slot_in_box < count, both[:, 128 * h : 128 * h + 128], 0.0
            )
    for c in table_copies + round1 + round2 + [up, down]:
        c.wait_send()


def shift_tiles():
    tiles = np.zeros((PAIRS, 8, 128), np.float32)
    for p in range(PAIRS):
        for c in range(3):
            tiles[p, c, :SLOTS] = SHIFTS[2 * p][c]
            tiles[p, c, SLOTS:] = SHIFTS[2 * p + 1][c]
    return tiles


def local_part(leaf_offsets, latent_charges, atom_counts, near_boxes, far_slots, branch_slots, far_operators):
    vmem = pl.BlockSpec(memory_space=pltpu.VMEM)
    smem = pl.BlockSpec(memory_space=pltpu.SMEM)
    sem = pltpu.SemaphoreType.DMA
    out = pl.pallas_call(
        kernel,
        out_shape=jax.ShapeDtypeStruct((1, ATOMS), F32),
        in_specs=[vmem, vmem, smem, smem, vmem, vmem, pl.BlockSpec(memory_space=pl.ANY), vmem],
        out_specs=vmem,
        scratch_shapes=[
            pltpu.VMEM((TERMS, LIST * TERMS), BF16),
            pltpu.VMEM((ROWS, ATOMS), F32),
            pltpu.VMEM((8, ATOMS), F32),
            pltpu.VMEM((EXT + 1, 8, 128), F32),
            pltpu.VMEM((ATOMS, 8), F32),
            pltpu.VMEM((ATOMS, 128), F32),
            pltpu.VMEM((1, 128), F32),
            pltpu.VMEM((2 * GROUP, 1, 128), F32),
            pltpu.VMEM((64, 128), BF16),
            pltpu.VMEM((4, 16, 128), BF16),
            pltpu.VMEM((4, 16, 128), BF16),
            pltpu.VMEM((GROUP - 1, 16, 128), BF16),
            pltpu.VMEM((GROUP - 1, 16, 128), BF16),
            pltpu.VMEM((96, 256), BF16),
            pltpu.VMEM((LIST * BOXES, 96), BF16),
            pltpu.VMEM((BOXES, 31360), BF16),
            pltpu.VMEM((BOXES, 128), F32),
            sem,
            sem((2 * GROUP,)),
            sem((2 * GROUP,)),
            sem((2,)),
            sem((2,)),
            sem((GROUP - 1,)),
            sem((GROUP - 1,)),
            sem((GROUP - 1,)),
            sem((GROUP - 1,)),
        ],
        compiler_params=pltpu.CompilerParams(
            collective_id=0, has_side_effects=True, vmem_limit_bytes=56 << 20
        ),
    )(
        leaf_offsets,
        latent_charges.reshape(1, ATOMS),
        atom_counts,
        near_boxes,
        far_slots,
        branch_slots,
        far_operators,
        shift_tiles(),
    )
    return out.reshape(-1)


def solution(mesh):
    boxes = ("gx", "gy", "gz")
    in_specs = (P(None, boxes), P(boxes), P(boxes), P(None, boxes), P(None, boxes), P(boxes, None, None), P())
    return jax.shard_map(local_part, mesh=mesh, in_specs=in_specs, out_specs=P(boxes), check_vma=False)
```

```python
import itertools

import jax
import jax.numpy as jnp
import numpy as np
from jax import lax
from jax.experimental import pallas as pl
from jax.experimental.pallas import tpu as pltpu
from jax.sharding import PartitionSpec as P

ORDER = 8
TERMS = 165
ROWS = 168
LIST = 189
BOXES = 32
SLOTS = 64
ATOMS = BOXES * SLOTS
HALO = 8
EXT = BOXES + 2 * HALO
SOFT2 = 0.0625
GROUP = 16
F32 = jnp.float32
BF16 = jnp.bfloat16
NT = (((1,), (1,)), ((), ()))
MESH = pl.DeviceIdType.MESH
SHIFTS = [s for s in itertools.product((-1, 0, 1), repeat=3) if s != (0, 0, 0)] + [(0, 0, 0)] * 2
PAIRS = len(SHIFTS) // 2


def degree_start(n):
    return n * (n + 1) * (n + 2) // 6


def low(m):
    return (m & -m).bit_length() - 1


def flipped(v, mask, bits):
    for b in range(bits):
        if mask >> b & 1:
            v = v + (1 << b) - (2 << b) * ((v // (1 << b)) % 2)
    return v


def partner(rnd, m):
    if rnd == 0:
        return {"gz": flipped(lax.axis_index("gz"), m, 4)}
    return {
        "gy": flipped(lax.axis_index("gy"), m & 3, 2),
        "gx": flipped(lax.axis_index("gx"), m >> 2, 2),
    }


def iota(shape, dim):
    return lax.broadcasted_iota(jnp.int32, shape, dim)


def fiota(shape, dim):
    return iota(shape, dim).astype(F32)


def split2(v):
    hi = v.astype(BF16)
    return hi, (v - hi.astype(F32)).astype(BF16)


def split3(v):
    hi = v.astype(BF16)
    rest = v - hi.astype(F32)
    mid = rest.astype(BF16)
    return hi, mid, (rest - mid.astype(F32)).astype(BF16)


def dot(a, b, dims=None):
    if dims is None:
        return jnp.dot(a, b, preferred_element_type=F32)
    return lax.dot_general(a, b, dims, preferred_element_type=F32)


def onehot(cond):
    return jnp.where(cond, 1.0, 0.0)


def main_tail_rows(cols, step, width):
    lanes = fiota((8, width), 1)
    rows = []
    for i in range(4):
        at = cols[8 * i : 8 * i + 8]
        rows.append(onehot(lanes == at))
        rows.append(onehot(lanes == at + step))
    return jnp.concatenate(rows, axis=0).astype(BF16)


def routed(tab_rows, tab_cols, base):
    lane = fiota((1, 128), 1)
    lane8 = (iota((1, 128), 1) % 8).astype(F32)
    sub = fiota((32, 1), 0)
    sub8 = (iota((32, 1), 0) % 8).astype(F32)

    def first_row(m):
        s = tab_rows[m : m + 1]
        return jnp.where(s < base, 16.0 * (m - 1) + lane8, 16.0 * m + s - base)

    def first_col(m):
        s = tab_cols[:32, m : m + 1]
        return jnp.where(s < base, 16.0 * (m - 1) + sub8, 16.0 * m + s - base)

    def looked_up(m, table_row, section):
        s = tab_cols[8 * section : 8 * section + 8, m : m + 1]
        lanes = fiota((8, 128), 1)
        found = jnp.sum(jnp.where(lanes == s - base, table_row, 0.0), axis=1, keepdims=True)
        return jnp.where(s < base, 16.0 * (m - 1) + sub8[:8], found)

    table4 = jnp.where(lane < 8, 16.0 * 4 + lane8, first_row(6))
    table12 = jnp.where(sub < 8, 16.0 * 12 + sub8, first_col(14))
    s12 = tab_rows[12:13]
    found12 = jnp.sum(jnp.where(fiota((32, 128), 0) == s12 - base, table12, 0.0), axis=0, keepdims=True)
    row12 = jnp.where(s12 < base, 16.0 * 11 + lane8, found12)
    table8 = jnp.where(lane < 8, 16.0 * 8 + lane8, jnp.where(lane < 16, first_row(10), row12))
    return jnp.concatenate(
        [sub8[:8], first_col(2)[8:16], looked_up(4, table4, 2), looked_up(8, table8, 3)], axis=0
    )


def stacked(*cases):
    row = iota((8, 128), 0)
    tiles = [
        jnp.where(row < 3, first, jnp.where(row == 3, third, jnp.where(row == 4, fourth, last)))
        for first, third, fourth, last in cases
    ]
    return jnp.concatenate(tiles, axis=0)


def norm_row(tile):
    square = tile * tile
    return square[0:1] + square[1:2] + square[2:3]


def target_rows(tile):
    row = iota((8, 128), 0)
    both = jnp.where(row == 4, norm_row(tile), jnp.where(row < 3, tile, pltpu.roll(tile, 5, 0)))
    u1, u2, u3 = (part.astype(F32) for part in split3(both))
    return stacked(
        (-2.0 * u1, 1.0, u1, 2.0),
        (-2.0 * u2, 0.0, u2, -2.0 * u1),
        (-2.0 * u3, 0.0, u3, -2.0 * u2),
        (-2.0 * u1, 1.0, 1.0, 2.0),
        (-2.0 * u2, 0.0, 0.0, -2.0 * u3),
        (-2.0 * u1, 1.0, 0.0, 2.0),
    )


def source_rows(tile):
    row = iota((8, 128), 0)
    both = jnp.where(row == 3, norm_row(tile) + SOFT2, jnp.where(row < 3, tile, pltpu.roll(tile, 5, 0)))
    s1, s2, s3 = (part.astype(F32) for part in split3(both))
    return stacked(
        (s1, s1, 1.0, s1),
        (s1, 0.0, 1.0, 1.0),
        (s1, 0.0, 1.0, 1.0),
        (s2, s2, 1.0, s2),
        (s2, 0.0, 0.0, 1.0),
        (s3, s3, 0.0, s3),
    )


def kernel(
    offs_ref, q_ref, counts_ref, near_ref, far_ref, branch_ref, op_hbm, factor_ref, out_ref,
    opv, tv, p8, dup, aims, sources, charges, accs, tabrow, tabs, own2, snd1, snd2, rcv1, rcv2, held, oh, col, tail,
    op_sem, tss, trs, hss, hrs, ss1, rs1, ss2, rs2,
):
    op_copy = pltpu.make_async_copy(op_hbm, opv, op_sem)
    op_copy.start()
    gz = lax.axis_index("gz")
    gzs = lax.axis_size("gz")
    barrier = pltpu.get_barrier_semaphore()
    for rnd in range(2):
        for m in range(1, GROUP):
            pl.semaphore_signal(barrier, inc=1, device_id=partner(rnd, m), device_id_type=MESH)

    lo8 = iota((8, 128), 1) < SLOTS
    slot_in_box = iota((1, 128), 1) % SLOTS
    lo1 = iota((1, 128), 1) < SLOTS
    p8[...] = jnp.zeros((8, ATOMS), F32)
    p8[0:3, :] = offs_ref[...]
    for r in range(BOXES // 2):
        count = jnp.where(lo1, counts_ref[2 * r], counts_ref[2 * r + 1])
        span = slice(128 * r, 128 * r + 128)
        p8[3:4, span] = jnp.where(slot_in_box < count, q_ref[:, span], 0.0)
    for r in range(BOXES // 2):
        span = slice(128 * r, 128 * r + 128)
        here = p8[:, span]
        other = pltpu.roll(here, SLOTS, 1)
        dup[HALO + 2 * r] = jnp.where(lo8, here, other)
        dup[HALO + 2 * r + 1] = jnp.where(lo8, other, here)
        aims[span, :] = jnp.transpose(target_rows(here)).astype(BF16)
    dup[EXT] = jnp.zeros((8, 128), F32)

    branch = branch_ref[0].astype(F32).astype(BF16)
    spread = onehot(iota((8, 128), 1) % 8 == iota((8, 128), 0)).astype(BF16)
    wide = dot(branch, spread)
    tabrow[...] = jnp.sum(
        jnp.where(iota((8, 128), 1) // 8 == iota((8, 128), 0), wide, 0.0), axis=0, keepdims=True
    )
    stretch = onehot(iota((64, 8), 0) // 8 == iota((64, 8), 1)).astype(BF16)
    tall = dot(stretch, branch)
    scol = jnp.sum(jnp.where(iota((64, 8), 1) == iota((64, 8), 0) % 8, tall, 0.0), axis=1, keepdims=True)

    def terms_block(blk, _):
        span = pl.ds(pl.multiple_of(blk * 256, 256), 256)
        x, y, z = (2.0 * p8[c : c + 1, span] for c in range(3))
        tv[0:1, span] = jnp.ones((1, 256), F32)
        for n in range(1, ORDER + 1):
            before, here, kept = degree_start(n - 1), degree_start(n), n * (n + 1) // 2
            tv[here : here + kept, span] = tv[before : before + kept, span] * x
            tv[here + kept : here + kept + n, span] = tv[before + kept - n : before + kept, span] * y
            tv[here + kept + n : here + kept + n + 1, span] = tv[before + kept - 1 : before + kept, span] * z
        tv[TERMS:ROWS, span] = jnp.zeros((ROWS - TERMS, 256), F32)
        return 0

    lax.fori_loop(0, ATOMS // 256, terms_block, 0)

    pl.semaphore_wait(barrier, 2 * (GROUP - 1))
    sends = []
    table_copies = []
    for rnd in range(2):
        for m in range(1, GROUP):
            at = rnd * GROUP + m
            c = pltpu.make_async_remote_copy(
                src_ref=tabrow, dst_ref=tabs.at[at], send_sem=tss.at[at], recv_sem=trs.at[at],
                device_id=partner(rnd, m), device_id_type=MESH,
            )
            c.start()
            table_copies.append(c)
    up = pltpu.make_async_remote_copy(
        src_ref=dup.at[pl.ds(BOXES, HALO)], dst_ref=dup.at[pl.ds(0, HALO)],
        send_sem=hss.at[0], recv_sem=hrs.at[0], device_id={"gz": (gz + 1) % gzs}, device_id_type=MESH,
    )
    down = pltpu.make_async_remote_copy(
        src_ref=dup.at[pl.ds(HALO, HALO)], dst_ref=dup.at[pl.ds(BOXES + HALO, HALO)],
        send_sem=hss.at[1], recv_sem=hrs.at[1], device_id={"gz": (gz + gzs - 1) % gzs}, device_id_type=MESH,
    )
    up.start()
    down.start()

    head = jnp.zeros((64, ROWS), F32)
    rest = jnp.zeros((32, ROWS), F32)
    for blk in range(ATOMS // 256):
        span = slice(256 * blk, 256 * blk + 256)
        mine = (256 * blk + iota((BOXES, 256), 1)) // SLOTS == iota((BOXES, 256), 0)
        qh, qm = split2(jnp.where(mine, p8[3:4, span], 0.0))
        th, tm = split2(tv[:, span])
        head = head + dot(jnp.concatenate([qh, qm], axis=0), th, NT)
        rest = rest + dot(qh, tm, NT)
    multipoles = head[:32] + head[32:] + rest
    tail[...] = jnp.zeros((32, 128), F32)
    tail[:, 0 : ROWS - 128] = multipoles[:, 128:ROWS]
    own_main = multipoles[:, 0:128].astype(BF16)
    own_tail = tail[...].astype(BF16)
    own2[0:32] = own_main
    own2[32:64] = own_tail
    held[0:32, 0:128] = own_main
    held[0:32, 128:256] = own_tail

    picked1 = jnp.where(scol[:32] < 32, scol[:32], -1000.0)
    snd1[...] = dot(main_tail_rows(picked1, 32.0, 64), own2[...]).astype(BF16).reshape(4, 16, 128)

    def exchange(rnd, snd, rcv, ss, rs):
        out = []
        for m in range(1, GROUP):
            c = pltpu.make_async_remote_copy(
                src_ref=snd.at[low(m)], dst_ref=rcv.at[m - 1], send_sem=ss.at[m - 1], recv_sem=rs.at[m - 1],
                device_id=partner(rnd, m), device_id_type=MESH,
            )
            c.start()
            out.append(c)
        return out

    round1 = exchange(0, snd1, rcv1, ss1, rs1)

    for c in table_copies:
        c.wait_recv()
    tabs[0] = tabrow[...]
    tabs[GROUP] = tabrow[...]
    rows1 = jnp.concatenate([tabs[m] for m in range(GROUP)], axis=0)
    rows2 = jnp.concatenate([tabs[GROUP + m] for m in range(GROUP)], axis=0)
    cols1 = jnp.transpose(jnp.concatenate([rows1, rows2] + [jnp.zeros((96, 128), F32)], axis=0))
    from1 = routed(rows1, cols1[0:32, 0:16], 32.0)
    from2 = routed(pltpu.roll(rows2, 96, 1), cols1[32:64, 16:32], 64.0)
    own_late = scol[32:64]
    fwd = onehot(fiota((32, 32), 1) == own_late - 32.0).astype(BF16)
    via = dot(fwd, jnp.broadcast_to(from1, (32, 128)).astype(BF16))[:, 0:1]
    late = jnp.where(jnp.logical_and(own_late >= 32, own_late < 64), via, -1000.0)
    lanes240 = fiota((32, 240), 1)
    select1 = jnp.concatenate(
        [
            main_tail_rows(late, 8.0, 240),
            onehot(lanes240 == from1).astype(BF16),
            onehot(lanes240 == from1 + 8.0).astype(BF16),
        ],
        axis=0,
    )
    select2 = jnp.concatenate(
        [onehot(lanes240 == from2).astype(BF16), onehot(lanes240 == from2 + 8.0).astype(BF16)], axis=0
    )
    picked2 = jnp.where(own_late < 32, own_late, -1000.0)
    from_own = dot(main_tail_rows(picked2, 32.0, 64), own2[...])

    up.wait_recv()
    down.wait_recv()
    base_box = (
        (lax.axis_index("gx") * lax.axis_size("gy") + lax.axis_index("gy")) * gzs + gz
    ) * BOXES - HALO

    for e in range(EXT + 1):
        tile = dup[e]
        sources[e] = source_rows(tile).astype(BF16)
        charges[e] = jnp.broadcast_to(tile[3:4], (8, 128))

    def near_box(g, _):
        lo = iota((8, 128), 1) < SLOTS
        lo48 = iota((48, 128), 1) < SLOTS
        at = pl.ds(pl.multiple_of(g * SLOTS, SLOTS), SLOTS)
        aim = aims[at, :]
        acc = [jnp.zeros((8, 128), F32) for _ in range(8)]
        for p0 in range(0, PAIRS, 2):
            there, weight = [], []
            for p in (p0, p0 + 1):
                if p < PAIRS - 1:
                    first, second = near_ref[2 * p, g], near_ref[2 * p + 1, g]
                    first = jnp.where(first < 0, EXT, jnp.clip(first - base_box, 0, EXT - 1))
                    second = jnp.where(second < 0, EXT, jnp.clip(second - base_box, 0, EXT - 1))
                else:
                    first, second = g + HALO, EXT
                there.append(jnp.where(lo48, sources[first], sources[second]) * factor_ref[p])
                weight.append(jnp.where(lo, charges[first], charges[second]))
            dist = dot(aim, jnp.concatenate(there, axis=1))
            for i in range(2):
                for k in range(8):
                    w = weight[i]
                    if p0 + i == PAIRS - 1:
                        w = jnp.where(iota((8, 128), 1) == 8 * k + iota((8, 128), 0), 0.0, w)
                    acc[k] = acc[k] + w * lax.rsqrt(dist[8 * k : 8 * k + 8, 128 * i : 128 * i + 128])
        accs[at, :] = jnp.concatenate(acc, axis=0)
        return 0

    lax.fori_loop(0, BOXES // 2, near_box, 0, unroll=8)

    for c in round1:
        c.wait_recv()
    got = dot(select1, rcv1[...].reshape(240, 128))
    snd2[...] = (got[0:64] + from_own).astype(BF16).reshape(4, 16, 128)
    round2 = exchange(1, snd2, rcv2, ss2, rs2)
    held[32:64, 0:128] = got[64:96].astype(BF16)
    held[32:64, 128:256] = got[96:128].astype(BF16)

    far_cols = far_ref[...].astype(F32)
    lanes96 = fiota((BOXES, 96), 1)
    for l in range(LIST):
        oh[BOXES * l : BOXES * l + BOXES, :] = onehot(lanes96 == far_cols[0:BOXES, l : l + 1]).astype(BF16)
    lax.fori_loop(BOXES // 2, BOXES, near_box, 0, unroll=8)
    ah, am = split2(accs[...])
    ones = jnp.ones((8, 128), BF16)
    near_row = (dot(ones, ah, NT) + dot(ones, am, NT))[0:1]

    for c in round2:
        c.wait_recv()
    got2 = dot(select2, rcv2[...].reshape(240, 128))
    held[64:96, 0:128] = got2[0:32].astype(BF16)
    held[64:96, 128:256] = got2[32:64].astype(BF16)

    table = held[...]

    for first in range(0, LIST, 8):
        count = min(8, LIST - first)
        some = dot(oh[BOXES * first : BOXES * (first + count), :], table).astype(BF16)
        for i in range(count):
            pos = (first + i) * TERMS
            col[:, pos : pos + TERMS] = some[BOXES * i : BOXES * i + BOXES, 0:TERMS]
    op_copy.wait()
    local = dot(opv[...], col[:, 0 : LIST * TERMS], NT)

    l1, l2, l3 = split3(local)
    parts = jnp.concatenate([l1.astype(F32), l2.astype(F32), l3.astype(F32)], axis=1).astype(BF16)
    for blk in range(ATOMS // 256):
        span = slice(256 * blk, 256 * blk + 256)
        boxes = onehot((256 * blk + iota((96, 256), 1)) // SLOTS == iota((96, 256), 0) % BOXES).astype(BF16)
        there = dot(parts, boxes)
        far = jnp.sum(there * tv[0:TERMS, span], axis=0, keepdims=True)
        both = far + near_row[:, span]
        for h in range(2):
            r = 2 * blk + h
            count = jnp.where(lo1, counts_ref[2 * r], counts_ref[2 * r + 1])
            out_ref[:, 128 * r : 128 * r + 128] = jnp.where(
                slot_in_box < count, both[:, 128 * h : 128 * h + 128], 0.0
            )
    for c in table_copies + round1 + round2 + [up, down]:
        c.wait_send()


def factor_tiles():
    tiles = np.ones((PAIRS, 6, 8, 128), np.float32)
    for p in range(PAIRS):
        for half in range(2):
            shift = SHIFTS[2 * p + half]
            lanes = slice(SLOTS * half, SLOTS * half + SLOTS)
            for c in range(3):
                tiles[p, :, 5 + c, lanes] = shift[c]
            tiles[p, 3, 4, lanes] = sum(c * c for c in shift)
    return tiles.reshape(PAIRS, 48, 128).astype(BF16)


def local_part(leaf_offsets, latent_charges, atom_counts, near_boxes, far_slots, branch_slots, far_operators):
    vmem = pl.BlockSpec(memory_space=pltpu.VMEM)
    smem = pl.BlockSpec(memory_space=pltpu.SMEM)
    sem = pltpu.SemaphoreType.DMA
    out = pl.pallas_call(
        kernel,
        out_shape=jax.ShapeDtypeStruct((1, ATOMS), F32),
        in_specs=[vmem, vmem, smem, smem, vmem, vmem, pl.BlockSpec(memory_space=pl.ANY), vmem],
        out_specs=vmem,
        scratch_shapes=[
            pltpu.VMEM((TERMS, LIST * TERMS), BF16),
            pltpu.VMEM((ROWS, ATOMS), F32),
            pltpu.VMEM((8, ATOMS), F32),
            pltpu.VMEM((EXT + 1, 8, 128), F32),
            pltpu.VMEM((ATOMS, 48), BF16),
            pltpu.VMEM((EXT + 1, 48, 128), BF16),
            pltpu.VMEM((EXT + 1, 8, 128), F32),
            pltpu.VMEM((ATOMS, 128), F32),
            pltpu.VMEM((1, 128), F32),
            pltpu.VMEM((2 * GROUP, 1, 128), F32),
            pltpu.VMEM((64, 128), BF16),
            pltpu.VMEM((4, 16, 128), BF16),
            pltpu.VMEM((4, 16, 128), BF16),
            pltpu.VMEM((GROUP - 1, 16, 128), BF16),
            pltpu.VMEM((GROUP - 1, 16, 128), BF16),
            pltpu.VMEM((96, 256), BF16),
            pltpu.VMEM((LIST * BOXES, 96), BF16),
            pltpu.VMEM((BOXES, 31232), BF16),
            pltpu.VMEM((BOXES, 128), F32),
            sem,
            sem((2 * GROUP,)),
            sem((2 * GROUP,)),
            sem((2,)),
            sem((2,)),
            sem((GROUP - 1,)),
            sem((GROUP - 1,)),
            sem((GROUP - 1,)),
            sem((GROUP - 1,)),
        ],
        compiler_params=pltpu.CompilerParams(
            collective_id=0, has_side_effects=True, vmem_limit_bytes=56 << 20
        ),
    )(
        leaf_offsets,
        latent_charges.reshape(1, ATOMS),
        atom_counts,
        near_boxes,
        far_slots.T,
        branch_slots,
        far_operators,
        factor_tiles(),
    )
    return out.reshape(-1)


def solution(mesh):
    boxes = ("gx", "gy", "gz")
    in_specs = (P(None, boxes), P(boxes), P(boxes), P(None, boxes), P(None, boxes), P(boxes, None, None), P())
    return jax.shard_map(local_part, mesh=mesh, in_specs=in_specs, out_specs=P(boxes), check_vma=False)
```

```python
import itertools

import jax
import jax.numpy as jnp
import numpy as np
from jax import lax
from jax.experimental import pallas as pl
from jax.experimental.pallas import tpu as pltpu
from jax.sharding import PartitionSpec as P

ORDER = 8
TERMS = 165
ROWS = 168
LIST = 189
BOXES = 32
SLOTS = 64
ATOMS = BOXES * SLOTS
HALO = 8
EXT = BOXES + 2 * HALO
SOFT2 = 0.0625
GROUP = 16
F32 = jnp.float32
BF16 = jnp.bfloat16
NT = (((1,), (1,)), ((), ()))
MESH = pl.DeviceIdType.MESH
SHIFTS = [s for s in itertools.product((-1, 0, 1), repeat=3) if s != (0, 0, 0)] + [(0, 0, 0)] * 2
PAIRS = len(SHIFTS) // 2


def degree_start(n):
    return n * (n + 1) * (n + 2) // 6


def low(m):
    return (m & -m).bit_length() - 1


def flipped(v, mask, bits):
    for b in range(bits):
        if mask >> b & 1:
            v = v + (1 << b) - (2 << b) * ((v // (1 << b)) % 2)
    return v


def partner(rnd, m):
    if rnd == 0:
        return {"gz": flipped(lax.axis_index("gz"), m, 4)}
    return {
        "gy": flipped(lax.axis_index("gy"), m & 3, 2),
        "gx": flipped(lax.axis_index("gx"), m >> 2, 2),
    }


def iota(shape, dim):
    return lax.broadcasted_iota(jnp.int32, shape, dim)


def fiota(shape, dim):
    return iota(shape, dim).astype(F32)


def split2(v):
    hi = v.astype(BF16)
    return hi, (v - hi.astype(F32)).astype(BF16)


def split3(v):
    hi = v.astype(BF16)
    rest = v - hi.astype(F32)
    mid = rest.astype(BF16)
    return hi, mid, (rest - mid.astype(F32)).astype(BF16)


def dot(a, b, dims=None):
    if dims is None:
        return jnp.dot(a, b, preferred_element_type=F32)
    return lax.dot_general(a, b, dims, preferred_element_type=F32)


def onehot(cond):
    return jnp.where(cond, 1.0, 0.0)


def main_tail_rows(cols, step, width):
    lanes = fiota((8, width), 1)
    rows = []
    for i in range(4):
        at = cols[8 * i : 8 * i + 8]
        rows.append(onehot(lanes == at))
        rows.append(onehot(lanes == at + step))
    return jnp.concatenate(rows, axis=0).astype(BF16)


def routed(got, rnd):
    base = 32.0 * (rnd + 1)
    lane = fiota((1, 128), 1)
    lane8 = (iota((1, 128), 1) % 8).astype(F32)
    sub8 = fiota((8, 1), 0)

    def named(m):
        return got[m - 1].astype(F32)[8:16]

    def as_row(m):
        return pltpu.roll(named(m), 32, 1)[0:1]

    def as_col(m, section):
        at = 64 + 4 * rnd + section
        return named(m)[:, at : at + 1]

    def first_row(m):
        s = as_row(m)
        return jnp.where(s < base, 16.0 * (m - 1) + lane8, 16.0 * m + s - base)

    def first_col(m):
        s = as_col(m, 1)
        return jnp.where(s < base, 16.0 * (m - 1) + sub8, 16.0 * m + s - base)

    def looked_up(m, table_row, section):
        s = as_col(m, section)
        found = jnp.sum(jnp.where(fiota((8, 128), 1) == s - base, table_row, 0.0), axis=1, keepdims=True)
        return jnp.where(s < base, 16.0 * (m - 1) + sub8, found)

    table4 = jnp.where(lane < 8, 16.0 * 4 + lane8, first_row(6))
    s12 = as_row(12)
    at12 = s12 - base
    found12 = jnp.sum(jnp.where(fiota((8, 128), 0) == at12 - 8.0, first_col(14), 0.0), axis=0, keepdims=True)
    found12 = jnp.where(at12 < 8, 16.0 * 12 + at12, found12)
    row12 = jnp.where(at12 < 0, 16.0 * 11 + lane8, found12)
    table8 = jnp.where(lane < 8, 16.0 * 8 + lane8, jnp.where(lane < 16, first_row(10), row12))
    return jnp.concatenate([sub8, first_col(2), looked_up(4, table4, 2), looked_up(8, table8, 3)], axis=0)


def stacked(*cases):
    row = iota((8, 128), 0)
    tiles = [
        jnp.where(row < 3, first, jnp.where(row == 3, third, jnp.where(row == 4, fourth, last)))
        for first, third, fourth, last in cases
    ]
    return jnp.concatenate(tiles, axis=0)


def norm_row(tile):
    square = tile * tile
    return square[0:1] + square[1:2] + square[2:3]


def target_rows(tile):
    row = iota((8, 128), 0)
    both = jnp.where(row == 4, norm_row(tile), jnp.where(row < 3, tile, pltpu.roll(tile, 5, 0)))
    u1, u2, u3 = (part.astype(F32) for part in split3(both))
    return stacked(
        (-2.0 * u1, 1.0, u1, 2.0),
        (-2.0 * u2, 0.0, u2, -2.0 * u1),
        (-2.0 * u3, 0.0, u3, -2.0 * u2),
        (-2.0 * u1, 1.0, 1.0, 2.0),
        (-2.0 * u2, 0.0, 0.0, -2.0 * u3),
        (-2.0 * u1, 1.0, 0.0, 2.0),
    )


def source_rows(tile):
    row = iota((8, 128), 0)
    both = jnp.where(row == 3, norm_row(tile) + SOFT2, jnp.where(row < 3, tile, pltpu.roll(tile, 5, 0)))
    s1, s2, s3 = (part.astype(F32) for part in split3(both))
    return stacked(
        (s1, s1, 1.0, s1),
        (s1, 0.0, 1.0, 1.0),
        (s1, 0.0, 1.0, 1.0),
        (s2, s2, 1.0, s2),
        (s2, 0.0, 0.0, 1.0),
        (s3, s3, 0.0, s3),
    )


def kernel(
    offs_ref, q_ref, counts_ref, near_hbm, far_hbm, branch_ref, op_hbm, factor_hbm, out_ref,
    opv, tv, p8, dup, aims, sources, charges, accs, near_ref, far_ref, factor_ref, own2, snd1, snd2, rcv1, rcv2, held, oh, col, tail,
    op_sem, in_sems, hss, hrs, ss1, rs1, ss2, rs2,
):
    loads = [
        pltpu.make_async_copy(src, dst, in_sems.at[i])
        for i, (src, dst) in enumerate(((far_hbm, far_ref), (near_hbm, near_ref), (factor_hbm, factor_ref)))
    ]
    for c in loads:
        c.start()
    op_copy = pltpu.make_async_copy(op_hbm, opv, op_sem)
    op_copy.start()
    gz = lax.axis_index("gz")
    gzs = lax.axis_size("gz")
    barrier = pltpu.get_barrier_semaphore()
    for rnd in range(2):
        for m in range(1, GROUP):
            pl.semaphore_signal(barrier, inc=1, device_id=partner(rnd, m), device_id_type=MESH)

    lo8 = iota((8, 128), 1) < SLOTS
    slot_in_box = iota((1, 128), 1) % SLOTS
    lo1 = iota((1, 128), 1) < SLOTS
    p8[...] = jnp.zeros((8, ATOMS), F32)
    p8[0:3, :] = offs_ref[...]
    for r in range(BOXES // 2):
        count = jnp.where(lo1, counts_ref[2 * r], counts_ref[2 * r + 1])
        span = slice(128 * r, 128 * r + 128)
        p8[3:4, span] = jnp.where(slot_in_box < count, q_ref[:, span], 0.0)
    for r in range(BOXES // 2):
        span = slice(128 * r, 128 * r + 128)
        here = p8[:, span]
        other = pltpu.roll(here, SLOTS, 1)
        dup[HALO + 2 * r] = jnp.where(lo8, here, other)
        dup[HALO + 2 * r + 1] = jnp.where(lo8, other, here)
        aims[span, :] = jnp.transpose(target_rows(here)).astype(BF16)
    dup[EXT] = jnp.zeros((8, 128), F32)

    branch = branch_ref[0].astype(F32).astype(BF16)
    spread = onehot(iota((8, 128), 1) % 8 == iota((8, 128), 0)).astype(BF16)
    wide = dot(branch, spread)
    own_row = jnp.sum(
        jnp.where(iota((8, 128), 1) // 8 == iota((8, 128), 0), wide, 0.0), axis=0, keepdims=True
    )
    stretch = onehot(iota((64, 8), 0) // 8 == iota((64, 8), 1)).astype(BF16)
    tall = dot(stretch, branch)
    scol = jnp.sum(jnp.where(iota((64, 8), 1) == iota((64, 8), 0) % 8, tall, 0.0), axis=1, keepdims=True)

    def named_tile(rnd):
        lanes = iota((8, 128), 1)
        tile = jnp.where(lanes >= 96, pltpu.roll(jnp.broadcast_to(own_row, (8, 128)), 96 - 32 * rnd, 1), 0.0)
        for i in range(4 * rnd, 4 * rnd + 4):
            tile = jnp.where(lanes == 64 + i, scol[8 * i : 8 * i + 8], tile)
        none = jnp.zeros((8, 128), F32)
        return jnp.concatenate([none, tile] * 4, axis=0)

    def terms_block(blk, _):
        span = pl.ds(pl.multiple_of(blk * 256, 256), 256)
        x, y, z = (2.0 * p8[c : c + 1, span] for c in range(3))
        tv[0:1, span] = jnp.ones((1, 256), F32)
        for n in range(1, ORDER + 1):
            before, here, kept = degree_start(n - 1), degree_start(n), n * (n + 1) // 2
            tv[here : here + kept, span] = tv[before : before + kept, span] * x
            tv[here + kept : here + kept + n, span] = tv[before + kept - n : before + kept, span] * y
            tv[here + kept + n : here + kept + n + 1, span] = tv[before + kept - 1 : before + kept, span] * z
        tv[TERMS:ROWS, span] = jnp.zeros((ROWS - TERMS, 256), F32)
        return 0

    lax.fori_loop(0, ATOMS // 256, terms_block, 0)

    head = jnp.zeros((64, ROWS), F32)
    rest = jnp.zeros((32, ROWS), F32)
    for blk in range(ATOMS // 256):
        span = slice(256 * blk, 256 * blk + 256)
        mine = (256 * blk + iota((BOXES, 256), 1)) // SLOTS == iota((BOXES, 256), 0)
        qh, qm = split2(jnp.where(mine, p8[3:4, span], 0.0))
        th, tm = split2(tv[:, span])
        head = head + dot(jnp.concatenate([qh, qm], axis=0), th, NT)
        rest = rest + dot(qh, tm, NT)
    multipoles = head[:32] + head[32:] + rest
    tail[...] = jnp.zeros((32, 128), F32)
    tail[:, 0 : ROWS - 128] = multipoles[:, 128:ROWS]
    own_main = multipoles[:, 0:128].astype(BF16)
    own_tail = tail[...].astype(BF16)
    own2[0:32] = own_main
    own2[32:64] = own_tail
    held[0:32, 0:128] = own_main
    held[0:32, 128:256] = own_tail

    picked1 = jnp.where(scol[:32] < 32, scol[:32], -1000.0)
    first_payload = dot(main_tail_rows(picked1, 32.0, 64), own2[...]) + named_tile(0)
    snd1[...] = first_payload.astype(BF16).reshape(4, 16, 128)
    second_names = named_tile(1)

    def exchange(rnd, snd, rcv, ss, rs):
        out = []
        for m in range(1, GROUP):
            c = pltpu.make_async_remote_copy(
                src_ref=snd.at[low(m)], dst_ref=rcv.at[m - 1], send_sem=ss.at[m - 1], recv_sem=rs.at[m - 1],
                device_id=partner(rnd, m), device_id_type=MESH,
            )
            c.start()
            out.append(c)
        return out

    pl.semaphore_wait(barrier, 2 * (GROUP - 1))
    round1 = exchange(0, snd1, rcv1, ss1, rs1)
    up = pltpu.make_async_remote_copy(
        src_ref=dup.at[pl.ds(BOXES, HALO)], dst_ref=dup.at[pl.ds(0, HALO)],
        send_sem=hss.at[0], recv_sem=hrs.at[0], device_id={"gz": (gz + 1) % gzs}, device_id_type=MESH,
    )
    down = pltpu.make_async_remote_copy(
        src_ref=dup.at[pl.ds(HALO, HALO)], dst_ref=dup.at[pl.ds(BOXES + HALO, HALO)],
        send_sem=hss.at[1], recv_sem=hrs.at[1], device_id={"gz": (gz + gzs - 1) % gzs}, device_id_type=MESH,
    )
    up.start()
    down.start()

    own_late = scol[32:64]
    picked2 = jnp.where(own_late < 32, own_late, -1000.0)
    from_own = dot(main_tail_rows(picked2, 32.0, 64), own2[...]) + second_names
    fwd = onehot(fiota((32, 32), 1) == own_late - 32.0).astype(BF16)
    loads[0].wait()
    far_cols = far_ref[...].astype(F32).astype(BF16)
    lanes96 = fiota((BOXES, 96), 1).astype(BF16)
    for l in range(LIST):
        here = jnp.where(lanes96 == far_cols[:, l : l + 1], jnp.ones((), BF16), jnp.zeros((), BF16))
        oh[BOXES * l : BOXES * l + BOXES, :] = here

    base_box = (
        (lax.axis_index("gx") * lax.axis_size("gy") + lax.axis_index("gy")) * gzs + gz
    ) * BOXES - HALO

    def prepare(e):
        tile = dup[e]
        sources[e] = source_rows(tile).astype(BF16)
        charges[e] = jnp.broadcast_to(tile[3:4], (8, 128))

    for e in list(range(HALO, BOXES + HALO)) + [EXT]:
        prepare(e)
    up.wait_recv()
    down.wait_recv()
    for e in list(range(HALO)) + list(range(BOXES + HALO, EXT)):
        prepare(e)
    loads[1].wait()
    loads[2].wait()

    def near_box(g, _):
        lo = iota((8, 128), 1) < SLOTS
        lo48 = iota((48, 128), 1) < SLOTS
        at = pl.ds(pl.multiple_of(g * SLOTS, SLOTS), SLOTS)
        aim = aims[at, :]
        acc = [jnp.zeros((8, 128), F32) for _ in range(8)]
        for p0 in range(0, PAIRS, 2):
            there, weight = [], []
            for p in (p0, p0 + 1):
                if p < PAIRS - 1:
                    first, second = near_ref[2 * p, g], near_ref[2 * p + 1, g]
                    first = jnp.where(first < 0, EXT, jnp.clip(first - base_box, 0, EXT - 1))
                    second = jnp.where(second < 0, EXT, jnp.clip(second - base_box, 0, EXT - 1))
                else:
                    first, second = g + HALO, EXT
                there.append(jnp.where(lo48, sources[first], sources[second]) * factor_ref[p])
                weight.append(jnp.where(lo, charges[first], charges[second]))
            dist = dot(aim, jnp.concatenate(there, axis=1))
            for i in range(2):
                for k in range(8):
                    w = weight[i]
                    if p0 + i == PAIRS - 1:
                        w = jnp.where(iota((8, 128), 1) == 8 * k + iota((8, 128), 0), 0.0, w)
                    acc[k] = acc[k] + w * lax.rsqrt(dist[8 * k : 8 * k + 8, 128 * i : 128 * i + 128])
        accs[at, :] = jnp.concatenate(acc, axis=0)
        return 0

    lax.fori_loop(0, 8, near_box, 0, unroll=8)

    for c in round1:
        c.wait_recv()
    lanes240 = fiota((32, 240), 1)
    from1 = routed(rcv1, 0)
    via = dot(fwd, jnp.broadcast_to(from1, (32, 128)).astype(BF16))[:, 0:1]
    late = jnp.where(jnp.logical_and(own_late >= 32, own_late < 64), via, -1000.0)
    select1 = jnp.concatenate(
        [
            main_tail_rows(late, 8.0, 240),
            onehot(lanes240 == from1).astype(BF16),
            onehot(lanes240 == from1 + 8.0).astype(BF16),
        ],
        axis=0,
    )
    got = dot(select1, rcv1[...].reshape(240, 128))
    is_tail = iota((64, 128), 0) % 16 >= 8
    passed_on = jnp.where(jnp.logical_and(is_tail, iota((64, 128), 1) >= 64), 0.0, got[0:64])
    snd2[...] = (passed_on + from_own).astype(BF16).reshape(4, 16, 128)
    round2 = exchange(1, snd2, rcv2, ss2, rs2)
    held[32:64, 0:128] = got[64:96].astype(BF16)
    held[32:64, 128:256] = got[96:128].astype(BF16)

    lax.fori_loop(8, BOXES, near_box, 0, unroll=8)
    ah, am = split2(accs[...])
    ones = jnp.ones((8, 128), BF16)
    near_row = (dot(ones, ah, NT) + dot(ones, am, NT))[0:1]

    for c in round2:
        c.wait_recv()
    from2 = routed(rcv2, 1)
    select2 = jnp.concatenate(
        [onehot(lanes240 == from2).astype(BF16), onehot(lanes240 == from2 + 8.0).astype(BF16)], axis=0
    )
    got2 = dot(select2, rcv2[...].reshape(240, 128))
    held[64:96, 0:128] = got2[0:32].astype(BF16)
    held[64:96, 128:256] = got2[32:64].astype(BF16)

    table = held[...]

    for first in range(0, LIST, 8):
        count = min(8, LIST - first)
        some = dot(oh[BOXES * first : BOXES * (first + count), :], table).astype(BF16)
        for i in range(count):
            pos = (first + i) * TERMS
            col[:, pos : pos + TERMS] = some[BOXES * i : BOXES * i + BOXES, 0:TERMS]
    op_copy.wait()
    local = dot(opv[...], col[:, 0 : LIST * TERMS], NT)

    l1, l2, l3 = split3(local)
    parts = jnp.concatenate([l1.astype(F32), l2.astype(F32), l3.astype(F32)], axis=1).astype(BF16)
    for blk in range(ATOMS // 256):
        span = slice(256 * blk, 256 * blk + 256)
        boxes = onehot((256 * blk + iota((96, 256), 1)) // SLOTS == iota((96, 256), 0) % BOXES).astype(BF16)
        there = dot(parts, boxes)
        far = jnp.sum(there * tv[0:TERMS, span], axis=0, keepdims=True)
        both = far + near_row[:, span]
        for h in range(2):
            r = 2 * blk + h
            count = jnp.where(lo1, counts_ref[2 * r], counts_ref[2 * r + 1])
            out_ref[:, 128 * r : 128 * r + 128] = jnp.where(
                slot_in_box < count, both[:, 128 * h : 128 * h + 128], 0.0
            )
    for c in round1 + round2 + [up, down]:
        c.wait_send()


def factor_tiles():
    tiles = np.ones((PAIRS, 6, 8, 128), np.float32)
    for p in range(PAIRS):
        for half in range(2):
            shift = SHIFTS[2 * p + half]
            lanes = slice(SLOTS * half, SLOTS * half + SLOTS)
            for c in range(3):
                tiles[p, :, 5 + c, lanes] = shift[c]
            tiles[p, 3, 4, lanes] = sum(c * c for c in shift)
    return tiles.reshape(PAIRS, 48, 128).astype(BF16)


def local_part(leaf_offsets, latent_charges, atom_counts, near_boxes, far_slots, branch_slots, far_operators):
    vmem = pl.BlockSpec(memory_space=pltpu.VMEM)
    smem = pl.BlockSpec(memory_space=pltpu.SMEM)
    hbm = pl.BlockSpec(memory_space=pl.ANY)
    sem = pltpu.SemaphoreType.DMA
    out = pl.pallas_call(
        kernel,
        out_shape=jax.ShapeDtypeStruct((1, ATOMS), F32),
        in_specs=[vmem, vmem, smem, hbm, hbm, vmem, hbm, hbm],
        out_specs=vmem,
        scratch_shapes=[
            pltpu.VMEM((TERMS, LIST * TERMS), BF16),
            pltpu.VMEM((ROWS, ATOMS), F32),
            pltpu.VMEM((8, ATOMS), F32),
            pltpu.VMEM((EXT + 1, 8, 128), F32),
            pltpu.VMEM((ATOMS, 48), BF16),
            pltpu.VMEM((EXT + 1, 48, 128), BF16),
            pltpu.VMEM((EXT + 1, 8, 128), F32),
            pltpu.VMEM((ATOMS, 128), F32),
            pltpu.SMEM((len(SHIFTS) - 2, BOXES), jnp.int32),
            pltpu.VMEM((BOXES, LIST), jnp.int32),
            pltpu.VMEM((PAIRS, 48, 128), BF16),
            pltpu.VMEM((64, 128), BF16),
            pltpu.VMEM((4, 16, 128), BF16),
            pltpu.VMEM((4, 16, 128), BF16),
            pltpu.VMEM((GROUP - 1, 16, 128), BF16),
            pltpu.VMEM((GROUP - 1, 16, 128), BF16),
            pltpu.VMEM((96, 256), BF16),
            pltpu.VMEM((LIST * BOXES, 96), BF16),
            pltpu.VMEM((BOXES, 31232), BF16),
            pltpu.VMEM((BOXES, 128), F32),
            sem,
            sem((3,)),
            sem((2,)),
            sem((2,)),
            sem((GROUP - 1,)),
            sem((GROUP - 1,)),
            sem((GROUP - 1,)),
            sem((GROUP - 1,)),
        ],
        compiler_params=pltpu.CompilerParams(
            collective_id=0, has_side_effects=True, vmem_limit_bytes=56 << 20
        ),
    )(
        leaf_offsets,
        latent_charges.reshape(1, ATOMS),
        atom_counts,
        near_boxes,
        far_slots.T,
        branch_slots,
        far_operators,
        factor_tiles(),
    )
    return out.reshape(-1)


def solution(mesh):
    boxes = ("gx", "gy", "gz")
    in_specs = (P(None, boxes), P(boxes), P(boxes), P(None, boxes), P(None, boxes), P(boxes, None, None), P())
    return jax.shard_map(local_part, mesh=mesh, in_specs=in_specs, out_specs=P(boxes), check_vma=False)
```

```python
import itertools

import jax
import jax.numpy as jnp
import numpy as np
from jax import lax
from jax.experimental import pallas as pl
from jax.experimental.pallas import tpu as pltpu
from jax.sharding import PartitionSpec as P

ORDER = 8
TERMS = 165
ROWS = 168
LIST = 189
BOXES = 32
SLOTS = 64
ATOMS = BOXES * SLOTS
HALO = 8
EXT = BOXES + 2 * HALO
SOFT2 = 0.0625
GROUP = 16
F32 = jnp.float32
BF16 = jnp.bfloat16
NT = (((1,), (1,)), ((), ()))
MESH = pl.DeviceIdType.MESH
SHIFTS = [s for s in itertools.product((-1, 0, 1), repeat=3) if s != (0, 0, 0)] + [(0, 0, 0)] * 2
PAIRS = len(SHIFTS) // 2
FARTHEST = (
    (8, 9, 10, 11, 6, 7, 12, 13, 4, 5, 14, 15, 2, 3, 1),
    (10, 6, 14, 9, 11, 2, 8, 5, 7, 13, 15, 1, 3, 4, 12),
)


def degree_start(n):
    return n * (n + 1) * (n + 2) // 6


def low(m):
    return (m & -m).bit_length() - 1


def flipped(v, mask, bits):
    for b in range(bits):
        if mask >> b & 1:
            v = v + (1 << b) - (2 << b) * ((v // (1 << b)) % 2)
    return v


def partner(rnd, m):
    if rnd == 0:
        return {"gz": flipped(lax.axis_index("gz"), m, 4)}
    return {
        "gy": flipped(lax.axis_index("gy"), m & 3, 2),
        "gx": flipped(lax.axis_index("gx"), m >> 2, 2),
    }


def iota(shape, dim):
    return lax.broadcasted_iota(jnp.int32, shape, dim)


def fiota(shape, dim):
    return iota(shape, dim).astype(F32)


def split2(v):
    hi = v.astype(BF16)
    return hi, (v - hi.astype(F32)).astype(BF16)


def split3(v):
    hi = v.astype(BF16)
    rest = v - hi.astype(F32)
    mid = rest.astype(BF16)
    return hi, mid, (rest - mid.astype(F32)).astype(BF16)


def dot(a, b, dims=None):
    if dims is None:
        return jnp.dot(a, b, preferred_element_type=F32)
    return lax.dot_general(a, b, dims, preferred_element_type=F32)


def onehot(cond):
    return jnp.where(cond, 1.0, 0.0)


def main_tail_rows(cols, step, width):
    lanes = fiota((8, width), 1)
    rows = []
    for i in range(4):
        at = cols[8 * i : 8 * i + 8]
        rows.append(onehot(lanes == at))
        rows.append(onehot(lanes == at + step))
    return jnp.concatenate(rows, axis=0).astype(BF16)


def routed(got, rnd):
    base = 32.0 * (rnd + 1)
    lane = fiota((1, 128), 1)
    lane8 = (iota((1, 128), 1) % 8).astype(F32)
    sub8 = fiota((8, 1), 0)

    def named(m):
        return got[m - 1].astype(F32)[8:16]

    def as_row(m):
        return pltpu.roll(named(m), 32, 1)[0:1]

    def as_col(m, section):
        at = 64 + 4 * rnd + section
        return named(m)[:, at : at + 1]

    def first_row(m):
        s = as_row(m)
        return jnp.where(s < base, 16.0 * (m - 1) + lane8, 16.0 * m + s - base)

    def first_col(m):
        s = as_col(m, 1)
        return jnp.where(s < base, 16.0 * (m - 1) + sub8, 16.0 * m + s - base)

    def looked_up(m, table_row, section):
        s = as_col(m, section)
        found = jnp.sum(jnp.where(fiota((8, 128), 1) == s - base, table_row, 0.0), axis=1, keepdims=True)
        return jnp.where(s < base, 16.0 * (m - 1) + sub8, found)

    table4 = jnp.where(lane < 8, 16.0 * 4 + lane8, first_row(6))
    s12 = as_row(12)
    at12 = s12 - base
    found12 = jnp.sum(jnp.where(fiota((8, 128), 0) == at12 - 8.0, first_col(14), 0.0), axis=0, keepdims=True)
    found12 = jnp.where(at12 < 8, 16.0 * 12 + at12, found12)
    row12 = jnp.where(at12 < 0, 16.0 * 11 + lane8, found12)
    table8 = jnp.where(lane < 8, 16.0 * 8 + lane8, jnp.where(lane < 16, first_row(10), row12))
    return jnp.concatenate([sub8, first_col(2), looked_up(4, table4, 2), looked_up(8, table8, 3)], axis=0)


def stacked(*cases):
    row = iota((8, 128), 0)
    tiles = [
        jnp.where(row < 3, first, jnp.where(row == 3, third, jnp.where(row == 4, fourth, last)))
        for first, third, fourth, last in cases
    ]
    return jnp.concatenate(tiles, axis=0)


def norm_row(tile):
    square = tile * tile
    return square[0:1] + square[1:2] + square[2:3]


def target_rows(tile):
    row = iota((8, 128), 0)
    both = jnp.where(row == 4, norm_row(tile), jnp.where(row < 3, tile, pltpu.roll(tile, 5, 0)))
    u1, u2, u3 = (part.astype(F32) for part in split3(both))
    return stacked(
        (-2.0 * u1, 1.0, u1, 2.0),
        (-2.0 * u2, 0.0, u2, -2.0 * u1),
        (-2.0 * u3, 0.0, u3, -2.0 * u2),
        (-2.0 * u1, 1.0, 1.0, 2.0),
        (-2.0 * u2, 0.0, 0.0, -2.0 * u3),
        (-2.0 * u1, 1.0, 0.0, 2.0),
    )


def source_rows(tile):
    row = iota((8, 128), 0)
    both = jnp.where(row == 3, norm_row(tile) + SOFT2, jnp.where(row < 3, tile, pltpu.roll(tile, 5, 0)))
    s1, s2, s3 = (part.astype(F32) for part in split3(both))
    return stacked(
        (s1, s1, 1.0, s1),
        (s1, 0.0, 1.0, 1.0),
        (s1, 0.0, 1.0, 1.0),
        (s2, s2, 1.0, s2),
        (s2, 0.0, 0.0, 1.0),
        (s3, s3, 0.0, s3),
    )


def kernel(
    offs_hbm, q_hbm, counts_hbm, near_hbm, far_hbm, branch_hbm, op_hbm, factor_hbm, near_out, far_out,
    opv, tv, p8, dup, aims, sources, charges, accs, offs_ref, q_ref, counts_ref, branch_ref, near_ref, far_ref, factor_ref, own2, snd1, snd2, rcv1, rcv2, held, oh, col, tail,
    op_sem, in_sems, hss, hrs, ss1, rs1, ss2, rs2,
):
    gz = lax.axis_index("gz")
    gzs = lax.axis_size("gz")
    barrier = pltpu.get_barrier_semaphore()
    loads = [
        pltpu.make_async_copy(src, dst, in_sems.at[i])
        for i, (src, dst) in enumerate(
            (
                (offs_hbm, offs_ref),
                (q_hbm, q_ref),
                (counts_hbm, counts_ref),
                (branch_hbm, branch_ref),
                (far_hbm, far_ref),
                (near_hbm, near_ref),
                (factor_hbm, factor_ref),
            )
        )
    ]
    for c in loads[:4]:
        c.start()
    for rnd in range(2):
        for m in FARTHEST[rnd]:
            pl.semaphore_signal(barrier, inc=1, device_id=partner(rnd, m), device_id_type=MESH)
    for c in loads[4:]:
        c.start()
    op_copy = pltpu.make_async_copy(op_hbm, opv, op_sem)
    op_copy.start()
    for c in loads[:4]:
        c.wait()

    lo8 = iota((8, 128), 1) < SLOTS
    slot_in_box = iota((1, 128), 1) % SLOTS
    lo1 = iota((1, 128), 1) < SLOTS
    p8[...] = jnp.zeros((8, ATOMS), F32)
    p8[0:3, :] = offs_ref[...]
    for r in range(BOXES // 2):
        count = jnp.where(lo1, counts_ref[2 * r], counts_ref[2 * r + 1])
        span = slice(128 * r, 128 * r + 128)
        p8[3:4, span] = jnp.where(slot_in_box < count, q_ref[:, span], 0.0)
    for r in range(BOXES // 2):
        span = slice(128 * r, 128 * r + 128)
        here = p8[:, span]
        other = pltpu.roll(here, SLOTS, 1)
        dup[HALO + 2 * r] = jnp.where(lo8, here, other)
        dup[HALO + 2 * r + 1] = jnp.where(lo8, other, here)
        aims[span, :] = jnp.transpose(target_rows(here)).astype(BF16)
    dup[EXT] = jnp.zeros((8, 128), F32)

    branch = branch_ref[0].astype(F32).astype(BF16)
    spread = onehot(iota((8, 128), 1) % 8 == iota((8, 128), 0)).astype(BF16)
    wide = dot(branch, spread)
    own_row = jnp.sum(
        jnp.where(iota((8, 128), 1) // 8 == iota((8, 128), 0), wide, 0.0), axis=0, keepdims=True
    )
    stretch = onehot(iota((64, 8), 0) // 8 == iota((64, 8), 1)).astype(BF16)
    tall = dot(stretch, branch)
    scol = jnp.sum(jnp.where(iota((64, 8), 1) == iota((64, 8), 0) % 8, tall, 0.0), axis=1, keepdims=True)

    def named_tile(rnd):
        lanes = iota((8, 128), 1)
        tile = jnp.where(lanes >= 96, pltpu.roll(jnp.broadcast_to(own_row, (8, 128)), 96 - 32 * rnd, 1), 0.0)
        for i in range(4 * rnd, 4 * rnd + 4):
            tile = jnp.where(lanes == 64 + i, scol[8 * i : 8 * i + 8], tile)
        none = jnp.zeros((8, 128), F32)
        return jnp.concatenate([none, tile] * 4, axis=0)

    def terms_block(blk, _):
        span = pl.ds(pl.multiple_of(blk * 256, 256), 256)
        x, y, z = (2.0 * p8[c : c + 1, span] for c in range(3))
        tv[0:1, span] = jnp.ones((1, 256), F32)
        for n in range(1, ORDER + 1):
            before, here, kept = degree_start(n - 1), degree_start(n), n * (n + 1) // 2
            tv[here : here + kept, span] = tv[before : before + kept, span] * x
            tv[here + kept : here + kept + n, span] = tv[before + kept - n : before + kept, span] * y
            tv[here + kept + n : here + kept + n + 1, span] = tv[before + kept - 1 : before + kept, span] * z
        tv[TERMS:ROWS, span] = jnp.zeros((ROWS - TERMS, 256), F32)
        return 0

    lax.fori_loop(0, ATOMS // 256, terms_block, 0)

    head = jnp.zeros((64, ROWS), F32)
    rest = jnp.zeros((32, ROWS), F32)
    for blk in range(ATOMS // 256):
        span = slice(256 * blk, 256 * blk + 256)
        mine = (256 * blk + iota((BOXES, 256), 1)) // SLOTS == iota((BOXES, 256), 0)
        qh, qm = split2(jnp.where(mine, p8[3:4, span], 0.0))
        th, tm = split2(tv[:, span])
        head = head + dot(jnp.concatenate([qh, qm], axis=0), th, NT)
        rest = rest + dot(qh, tm, NT)
    multipoles = head[:32] + head[32:] + rest
    tail[...] = jnp.zeros((32, 128), F32)
    tail[:, 0 : ROWS - 128] = multipoles[:, 128:ROWS]
    own_main = multipoles[:, 0:128].astype(BF16)
    own_tail = tail[...].astype(BF16)
    own2[0:32] = own_main
    own2[32:64] = own_tail
    held[0:32, 0:128] = own_main
    held[0:32, 128:256] = own_tail

    picked1 = jnp.where(scol[:32] < 32, scol[:32], -1000.0)
    first_payload = dot(main_tail_rows(picked1, 32.0, 64), own2[...]) + named_tile(0)
    snd1[...] = first_payload.astype(BF16).reshape(4, 16, 128)
    second_names = named_tile(1)

    def exchange(rnd, snd, rcv, ss, rs):
        out = []
        for m in FARTHEST[rnd]:
            c = pltpu.make_async_remote_copy(
                src_ref=snd.at[low(m)], dst_ref=rcv.at[m - 1], send_sem=ss.at[m - 1], recv_sem=rs.at[m - 1],
                device_id=partner(rnd, m), device_id_type=MESH,
            )
            c.start()
            out.append(c)
        return out

    pl.semaphore_wait(barrier, 2 * (GROUP - 1))
    round1 = exchange(0, snd1, rcv1, ss1, rs1)
    up = pltpu.make_async_remote_copy(
        src_ref=dup.at[pl.ds(BOXES, HALO)], dst_ref=dup.at[pl.ds(0, HALO)],
        send_sem=hss.at[0], recv_sem=hrs.at[0], device_id={"gz": (gz + 1) % gzs}, device_id_type=MESH,
    )
    down = pltpu.make_async_remote_copy(
        src_ref=dup.at[pl.ds(HALO, HALO)], dst_ref=dup.at[pl.ds(BOXES + HALO, HALO)],
        send_sem=hss.at[1], recv_sem=hrs.at[1], device_id={"gz": (gz + gzs - 1) % gzs}, device_id_type=MESH,
    )
    up.start()
    down.start()

    own_late = scol[32:64]
    picked2 = jnp.where(own_late < 32, own_late, -1000.0)
    from_own = dot(main_tail_rows(picked2, 32.0, 64), own2[...]) + second_names
    fwd = onehot(fiota((32, 32), 1) == own_late - 32.0).astype(BF16)
    loads[4].wait()
    far_cols = far_ref[...].astype(F32).astype(BF16)
    lanes96 = fiota((BOXES, 96), 1).astype(BF16)
    for l in range(LIST):
        here = jnp.where(lanes96 == far_cols[:, l : l + 1], jnp.ones((), BF16), jnp.zeros((), BF16))
        oh[BOXES * l : BOXES * l + BOXES, :] = here

    base_box = (
        (lax.axis_index("gx") * lax.axis_size("gy") + lax.axis_index("gy")) * gzs + gz
    ) * BOXES - HALO

    def prepare(e):
        tile = dup[e]
        sources[e] = source_rows(tile).astype(BF16)
        charges[e] = jnp.broadcast_to(tile[3:4], (8, 128))

    for e in list(range(HALO, BOXES + HALO)) + [EXT]:
        prepare(e)
    up.wait_recv()
    down.wait_recv()
    for e in list(range(HALO)) + list(range(BOXES + HALO, EXT)):
        prepare(e)
    loads[5].wait()
    loads[6].wait()

    def near_box(g, _):
        lo = iota((8, 128), 1) < SLOTS
        lo48 = iota((48, 128), 1) < SLOTS
        at = pl.ds(pl.multiple_of(g * SLOTS, SLOTS), SLOTS)
        aim = aims[at, :]
        acc = [jnp.zeros((8, 128), F32) for _ in range(8)]
        for p0 in range(0, PAIRS, 2):
            there, weight = [], []
            for p in (p0, p0 + 1):
                if p < PAIRS - 1:
                    first, second = near_ref[2 * p, g], near_ref[2 * p + 1, g]
                    first = jnp.where(first < 0, EXT, jnp.clip(first - base_box, 0, EXT - 1))
                    second = jnp.where(second < 0, EXT, jnp.clip(second - base_box, 0, EXT - 1))
                else:
                    first, second = g + HALO, EXT
                there.append(jnp.where(lo48, sources[first], sources[second]) * factor_ref[p])
                weight.append(jnp.where(lo, charges[first], charges[second]))
            dist = dot(aim, jnp.concatenate(there, axis=1))
            for i in range(2):
                for k in range(8):
                    w = weight[i]
                    if p0 + i == PAIRS - 1:
                        w = jnp.where(iota((8, 128), 1) == 8 * k + iota((8, 128), 0), 0.0, w)
                    acc[k] = acc[k] + w * lax.rsqrt(dist[8 * k : 8 * k + 8, 128 * i : 128 * i + 128])
        accs[at, :] = jnp.concatenate(acc, axis=0)
        return 0

    lax.fori_loop(0, 16, near_box, 0, unroll=8)

    for c in round1:
        c.wait_recv()
    lanes240 = fiota((32, 240), 1)
    from1 = routed(rcv1, 0)
    via = dot(fwd, jnp.broadcast_to(from1, (32, 128)).astype(BF16))[:, 0:1]
    late = jnp.where(jnp.logical_and(own_late >= 32, own_late < 64), via, -1000.0)
    select1 = jnp.concatenate(
        [
            main_tail_rows(late, 8.0, 240),
            onehot(lanes240 == from1).astype(BF16),
            onehot(lanes240 == from1 + 8.0).astype(BF16),
        ],
        axis=0,
    )
    got = dot(select1, rcv1[...].reshape(240, 128))
    is_tail = iota((64, 128), 0) % 16 >= 8
    passed_on = jnp.where(jnp.logical_and(is_tail, iota((64, 128), 1) >= 64), 0.0, got[0:64])
    snd2[...] = (passed_on + from_own).astype(BF16).reshape(4, 16, 128)
    round2 = exchange(1, snd2, rcv2, ss2, rs2)
    held[32:64, 0:128] = got[64:96].astype(BF16)
    held[32:64, 128:256] = got[96:128].astype(BF16)

    lax.fori_loop(16, BOXES, near_box, 0, unroll=8)
    ah, am = split2(accs[...])
    ones = jnp.ones((8, 128), BF16)
    near_row = (dot(ones, ah, NT) + dot(ones, am, NT))[0:1]
    for r in range(BOXES // 2):
        count = jnp.where(lo1, counts_ref[2 * r], counts_ref[2 * r + 1])
        near_out[r : r + 1, :] = jnp.where(slot_in_box < count, near_row[:, 128 * r : 128 * r + 128], 0.0)

    for c in round2:
        c.wait_recv()
    from2 = routed(rcv2, 1)
    select2 = jnp.concatenate(
        [onehot(lanes240 == from2).astype(BF16), onehot(lanes240 == from2 + 8.0).astype(BF16)], axis=0
    )
    got2 = dot(select2, rcv2[...].reshape(240, 128))
    held[64:96, 0:128] = got2[0:32].astype(BF16)
    held[64:96, 128:256] = got2[32:64].astype(BF16)

    table = held[...]

    for first in range(0, LIST, 8):
        count = min(8, LIST - first)
        some = dot(oh[BOXES * first : BOXES * (first + count), :], table).astype(BF16)
        for i in range(count):
            pos = (first + i) * TERMS
            col[:, pos : pos + TERMS] = some[BOXES * i : BOXES * i + BOXES, 0:TERMS]
    op_copy.wait()
    local = dot(opv[...], col[:, 0 : LIST * TERMS], NT)

    l1, l2, l3 = split3(local)
    parts = jnp.concatenate([l1.astype(F32), l2.astype(F32), l3.astype(F32)], axis=1).astype(BF16)
    for blk in range(ATOMS // 256):
        span = slice(256 * blk, 256 * blk + 256)
        boxes = onehot((256 * blk + iota((96, 256), 1)) // SLOTS == iota((96, 256), 0) % BOXES).astype(BF16)
        there = dot(parts, boxes)
        far = jnp.sum(there * tv[0:TERMS, span], axis=0, keepdims=True)
        for h in range(2):
            r = 2 * blk + h
            count = jnp.where(lo1, counts_ref[2 * r], counts_ref[2 * r + 1])
            far_out[r : r + 1, :] = jnp.where(slot_in_box < count, far[:, 128 * h : 128 * h + 128], 0.0)
    for c in round1 + round2 + [up, down]:
        c.wait_send()


def factor_tiles():
    tiles = np.ones((PAIRS, 6, 8, 128), np.float32)
    for p in range(PAIRS):
        for half in range(2):
            shift = SHIFTS[2 * p + half]
            lanes = slice(SLOTS * half, SLOTS * half + SLOTS)
            for c in range(3):
                tiles[p, :, 5 + c, lanes] = shift[c]
            tiles[p, 3, 4, lanes] = sum(c * c for c in shift)
    return tiles.reshape(PAIRS, 48, 128).astype(BF16)


def local_part(leaf_offsets, latent_charges, atom_counts, near_boxes, far_slots, branch_slots, far_operators):
    vmem = pl.BlockSpec(memory_space=pltpu.VMEM)
    hbm = pl.BlockSpec(memory_space=pl.ANY)
    sem = pltpu.SemaphoreType.DMA
    near, far = pl.pallas_call(
        kernel,
        out_shape=[jax.ShapeDtypeStruct((ATOMS // 128, 128), F32)] * 2,
        in_specs=[hbm] * 8,
        out_specs=[vmem, vmem],
        scratch_shapes=[
            pltpu.VMEM((TERMS, LIST * TERMS), BF16),
            pltpu.VMEM((ROWS, ATOMS), F32),
            pltpu.VMEM((8, ATOMS), F32),
            pltpu.VMEM((EXT + 1, 8, 128), F32),
            pltpu.VMEM((ATOMS, 48), BF16),
            pltpu.VMEM((EXT + 1, 48, 128), BF16),
            pltpu.VMEM((EXT + 1, 8, 128), F32),
            pltpu.VMEM((ATOMS, 128), F32),
            pltpu.VMEM((3, ATOMS), F32),
            pltpu.VMEM((1, ATOMS), F32),
            pltpu.SMEM((BOXES,), jnp.int32),
            pltpu.VMEM((1, 8, 8), jnp.int32),
            pltpu.SMEM((len(SHIFTS) - 2, BOXES), jnp.int32),
            pltpu.VMEM((BOXES, LIST), jnp.int32),
            pltpu.VMEM((PAIRS, 48, 128), BF16),
            pltpu.VMEM((64, 128), BF16),
            pltpu.VMEM((4, 16, 128), BF16),
            pltpu.VMEM((4, 16, 128), BF16),
            pltpu.VMEM((GROUP - 1, 16, 128), BF16),
            pltpu.VMEM((GROUP - 1, 16, 128), BF16),
            pltpu.VMEM((96, 256), BF16),
            pltpu.VMEM((LIST * BOXES, 96), BF16),
            pltpu.VMEM((BOXES, 31232), BF16),
            pltpu.VMEM((BOXES, 128), F32),
            sem,
            sem((7,)),
            sem((2,)),
            sem((2,)),
            sem((GROUP - 1,)),
            sem((GROUP - 1,)),
            sem((GROUP - 1,)),
            sem((GROUP - 1,)),
        ],
        compiler_params=pltpu.CompilerParams(
            collective_id=0, has_side_effects=True, vmem_limit_bytes=56 << 20
        ),
    )(
        leaf_offsets,
        latent_charges.reshape(1, ATOMS),
        atom_counts,
        near_boxes,
        far_slots.T,
        branch_slots,
        far_operators,
        factor_tiles(),
    )
    return (near + far).reshape(-1)


def solution(mesh):
    boxes = ("gx", "gy", "gz")
    in_specs = (P(None, boxes), P(boxes), P(boxes), P(None, boxes), P(None, boxes), P(boxes, None, None), P())
    return jax.shard_map(local_part, mesh=mesh, in_specs=in_specs, out_specs=P(boxes), check_vma=False)
```

```python
import itertools

import jax
import jax.numpy as jnp
import numpy as np
from jax import lax
from jax.experimental import pallas as pl
from jax.experimental.pallas import tpu as pltpu
from jax.sharding import PartitionSpec as P

ORDER = 8
TERMS = 165
ROWS = 168
LIST = 189
BOXES = 32
SLOTS = 64
ATOMS = BOXES * SLOTS
HALO = 8
EXT = BOXES + 2 * HALO
SOFT2 = 0.0625
GROUP = 16
F32 = jnp.float32
BF16 = jnp.bfloat16
NT = (((1,), (1,)), ((), ()))
MESH = pl.DeviceIdType.MESH
SHIFTS = [s for s in itertools.product((-1, 0, 1), repeat=3) if s != (0, 0, 0)] + [(0, 0, 0)] * 2
PAIRS = len(SHIFTS) // 2
FARTHEST = (
    (8, 9, 10, 11, 6, 7, 12, 13, 4, 5, 14, 15, 2, 3, 1),
    (10, 6, 14, 9, 11, 2, 8, 5, 7, 13, 15, 1, 3, 4, 12),
)


def degree_start(n):
    return n * (n + 1) * (n + 2) // 6


def low(m):
    return (m & -m).bit_length() - 1


def flips(axis, bits):
    at = lax.axis_index(axis)
    return [(1 << b) * (1 - 2 * lax.rem(lax.div(at, jnp.int32(1 << b)), jnp.int32(2))) for b in range(bits)]


def moved(axis, steps, mask):
    at = lax.axis_index(axis)
    for b, step in enumerate(steps):
        if mask >> b & 1:
            at = at + step
    return at


def iota(shape, dim):
    return lax.broadcasted_iota(jnp.int32, shape, dim)


def fiota(shape, dim):
    return iota(shape, dim).astype(F32)


def split2(v):
    hi = v.astype(BF16)
    return hi, (v - hi.astype(F32)).astype(BF16)


def split3(v):
    hi = v.astype(BF16)
    rest = v - hi.astype(F32)
    mid = rest.astype(BF16)
    return hi, mid, (rest - mid.astype(F32)).astype(BF16)


def dot(a, b, dims=None):
    if dims is None:
        return jnp.dot(a, b, preferred_element_type=F32)
    return lax.dot_general(a, b, dims, preferred_element_type=F32)


def onehot(cond):
    return jnp.where(cond, 1.0, 0.0)


def main_tail_rows(cols, step, width):
    lanes = fiota((8, width), 1)
    rows = []
    for i in range(4):
        at = cols[8 * i : 8 * i + 8]
        rows.append(onehot(lanes == at))
        rows.append(onehot(lanes == at + step))
    return jnp.concatenate(rows, axis=0).astype(BF16)


def routed(got, rnd):
    base = 32.0 * (rnd + 1)
    lane = fiota((1, 128), 1)
    lane8 = (iota((1, 128), 1) % 8).astype(F32)
    sub8 = fiota((8, 1), 0)

    def named(m):
        return got[m - 1].astype(F32)[8:16]

    def as_row(m):
        return pltpu.roll(named(m), 32, 1)[0:1]

    def as_col(m, section):
        at = 64 + 4 * rnd + section
        return named(m)[:, at : at + 1]

    def first_row(m):
        s = as_row(m)
        return jnp.where(s < base, 16.0 * (m - 1) + lane8, 16.0 * m + s - base)

    def first_col(m):
        s = as_col(m, 1)
        return jnp.where(s < base, 16.0 * (m - 1) + sub8, 16.0 * m + s - base)

    def looked_up(m, table_row, section):
        s = as_col(m, section)
        found = jnp.sum(jnp.where(fiota((8, 128), 1) == s - base, table_row, 0.0), axis=1, keepdims=True)
        return jnp.where(s < base, 16.0 * (m - 1) + sub8, found)

    table4 = jnp.where(lane < 8, 16.0 * 4 + lane8, first_row(6))
    s12 = as_row(12)
    at12 = s12 - base
    found12 = jnp.sum(jnp.where(fiota((8, 128), 0) == at12 - 8.0, first_col(14), 0.0), axis=0, keepdims=True)
    found12 = jnp.where(at12 < 8, 16.0 * 12 + at12, found12)
    row12 = jnp.where(at12 < 0, 16.0 * 11 + lane8, found12)
    table8 = jnp.where(lane < 8, 16.0 * 8 + lane8, jnp.where(lane < 16, first_row(10), row12))
    return jnp.concatenate([sub8, first_col(2), looked_up(4, table4, 2), looked_up(8, table8, 3)], axis=0)


def stacked(*cases):
    row = iota((8, 128), 0)
    tiles = [
        jnp.where(row < 3, first, jnp.where(row == 3, third, jnp.where(row == 4, fourth, last)))
        for first, third, fourth, last in cases
    ]
    return jnp.concatenate(tiles, axis=0)


def norm_row(tile):
    square = tile * tile
    return square[0:1] + square[1:2] + square[2:3]


def target_rows(tile):
    row = iota((8, 128), 0)
    both = jnp.where(row == 4, norm_row(tile), jnp.where(row < 3, tile, pltpu.roll(tile, 5, 0)))
    u1, u2, u3 = (part.astype(F32) for part in split3(both))
    return stacked(
        (-2.0 * u1, 1.0, u1, 2.0),
        (-2.0 * u2, 0.0, u2, -2.0 * u1),
        (-2.0 * u3, 0.0, u3, -2.0 * u2),
        (-2.0 * u1, 1.0, 1.0, 2.0),
        (-2.0 * u2, 0.0, 0.0, -2.0 * u3),
        (-2.0 * u1, 1.0, 0.0, 2.0),
    )


def source_rows(tile):
    row = iota((8, 128), 0)
    both = jnp.where(row == 3, norm_row(tile) + SOFT2, jnp.where(row < 3, tile, pltpu.roll(tile, 5, 0)))
    s1, s2, s3 = (part.astype(F32) for part in split3(both))
    return stacked(
        (s1, s1, 1.0, s1),
        (s1, 0.0, 1.0, 1.0),
        (s1, 0.0, 1.0, 1.0),
        (s2, s2, 1.0, s2),
        (s2, 0.0, 0.0, 1.0),
        (s3, s3, 0.0, s3),
    )


def kernel(
    offs_hbm, q_hbm, counts_hbm, near_hbm, far_hbm, branch_hbm, op_hbm, factor_hbm, near_out, far_out,
    opv, tv, p8, dup, aims, sources, charges, accs, offs_ref, q_ref, counts_ref, branch_ref, near_ref, far_ref, factor_ref, own2, snd1, snd2, rcv1, rcv2, held, oh, col, tail,
    op_sem, in_sems, hss, hrs, ss1, rs1, ss2, rs2,
):
    gz = lax.axis_index("gz")
    gzs = lax.axis_size("gz")
    z_flips, y_flips, x_flips = flips("gz", 4), flips("gy", 2), flips("gx", 2)
    at_gz = [{"gz": moved("gz", z_flips, m)} for m in range(GROUP)]
    at_gy = [moved("gy", y_flips, m) for m in range(4)]
    at_gx = [moved("gx", x_flips, m) for m in range(4)]
    partners = (at_gz, [{"gy": at_gy[m & 3], "gx": at_gx[m >> 2]} for m in range(GROUP)])
    barrier = pltpu.get_barrier_semaphore()
    loads = [
        pltpu.make_async_copy(src, dst, in_sems.at[i])
        for i, (src, dst) in enumerate(
            (
                (offs_hbm, offs_ref),
                (q_hbm, q_ref),
                (counts_hbm, counts_ref),
                (branch_hbm, branch_ref),
                (far_hbm, far_ref),
                (near_hbm, near_ref),
                (factor_hbm, factor_ref),
            )
        )
    ]
    for c in loads[:4]:
        c.start()
    for rnd in range(2):
        for m in FARTHEST[rnd]:
            pl.semaphore_signal(barrier, inc=1, device_id=partners[rnd][m], device_id_type=MESH)
    for c in loads[4:]:
        c.start()
    op_copy = pltpu.make_async_copy(op_hbm, opv, op_sem)
    op_copy.start()
    for c in loads[:4]:
        c.wait()

    lo8 = iota((8, 128), 1) < SLOTS
    slot_in_box = iota((1, 128), 1) % SLOTS
    lo1 = iota((1, 128), 1) < SLOTS
    p8[...] = jnp.zeros((8, ATOMS), F32)
    p8[0:3, :] = offs_ref[...]
    for r in range(BOXES // 2):
        count = jnp.where(lo1, counts_ref[2 * r], counts_ref[2 * r + 1])
        span = slice(128 * r, 128 * r + 128)
        p8[3:4, span] = jnp.where(slot_in_box < count, q_ref[:, span], 0.0)
    for r in range(BOXES // 2):
        span = slice(128 * r, 128 * r + 128)
        here = p8[:, span]
        other = pltpu.roll(here, SLOTS, 1)
        dup[HALO + 2 * r] = jnp.where(lo8, here, other)
        dup[HALO + 2 * r + 1] = jnp.where(lo8, other, here)
        aims[span, :] = jnp.transpose(target_rows(here)).astype(BF16)
    dup[EXT] = jnp.zeros((8, 128), F32)

    branch = branch_ref[0].astype(F32).astype(BF16)
    spread = onehot(iota((8, 128), 1) % 8 == iota((8, 128), 0)).astype(BF16)
    wide = dot(branch, spread)
    own_row = jnp.sum(
        jnp.where(iota((8, 128), 1) // 8 == iota((8, 128), 0), wide, 0.0), axis=0, keepdims=True
    )
    stretch = onehot(iota((64, 8), 0) // 8 == iota((64, 8), 1)).astype(BF16)
    tall = dot(stretch, branch)
    scol = jnp.sum(jnp.where(iota((64, 8), 1) == iota((64, 8), 0) % 8, tall, 0.0), axis=1, keepdims=True)

    def named_tile(rnd):
        lanes = iota((8, 128), 1)
        tile = jnp.where(lanes >= 96, pltpu.roll(jnp.broadcast_to(own_row, (8, 128)), 96 - 32 * rnd, 1), 0.0)
        for i in range(4 * rnd, 4 * rnd + 4):
            tile = jnp.where(lanes == 64 + i, scol[8 * i : 8 * i + 8], tile)
        none = jnp.zeros((8, 128), F32)
        return jnp.concatenate([none, tile] * 4, axis=0)

    def terms_block(blk, _):
        span = pl.ds(pl.multiple_of(blk * 256, 256), 256)
        x, y, z = (2.0 * p8[c : c + 1, span] for c in range(3))
        tv[0:1, span] = jnp.ones((1, 256), F32)
        for n in range(1, ORDER + 1):
            before, here, kept = degree_start(n - 1), degree_start(n), n * (n + 1) // 2
            tv[here : here + kept, span] = tv[before : before + kept, span] * x
            tv[here + kept : here + kept + n, span] = tv[before + kept - n : before + kept, span] * y
            tv[here + kept + n : here + kept + n + 1, span] = tv[before + kept - 1 : before + kept, span] * z
        tv[TERMS:ROWS, span] = jnp.zeros((ROWS - TERMS, 256), F32)
        return 0

    lax.fori_loop(0, ATOMS // 256, terms_block, 0)

    head = jnp.zeros((64, ROWS), F32)
    rest = jnp.zeros((32, ROWS), F32)
    for blk in range(ATOMS // 256):
        span = slice(256 * blk, 256 * blk + 256)
        mine = (256 * blk + iota((BOXES, 256), 1)) // SLOTS == iota((BOXES, 256), 0)
        qh, qm = split2(jnp.where(mine, p8[3:4, span], 0.0))
        th, tm = split2(tv[:, span])
        head = head + dot(jnp.concatenate([qh, qm], axis=0), th, NT)
        rest = rest + dot(qh, tm, NT)
    multipoles = head[:32] + head[32:] + rest
    tail[...] = jnp.zeros((32, 128), F32)
    tail[:, 0 : ROWS - 128] = multipoles[:, 128:ROWS]
    own_main = multipoles[:, 0:128].astype(BF16)
    own_tail = tail[...].astype(BF16)
    own2[0:32] = own_main
    own2[32:64] = own_tail
    held[0:32, 0:128] = own_main
    held[0:32, 128:256] = own_tail

    picked1 = jnp.where(scol[:32] < 32, scol[:32], -1000.0)
    first_payload = dot(main_tail_rows(picked1, 32.0, 64), own2[...]) + named_tile(0)
    snd1[...] = first_payload.astype(BF16).reshape(4, 16, 128)
    second_names = named_tile(1)

    def exchange(rnd, snd, rcv, ss, rs):
        out = []
        for m in FARTHEST[rnd]:
            c = pltpu.make_async_remote_copy(
                src_ref=snd.at[low(m)], dst_ref=rcv.at[m - 1], send_sem=ss.at[m - 1], recv_sem=rs.at[m - 1],
                device_id=partners[rnd][m], device_id_type=MESH,
            )
            c.start()
            out.append(c)
        return out

    pl.semaphore_wait(barrier, 2 * (GROUP - 1))
    round1 = exchange(0, snd1, rcv1, ss1, rs1)
    up = pltpu.make_async_remote_copy(
        src_ref=dup.at[pl.ds(BOXES, HALO)], dst_ref=dup.at[pl.ds(0, HALO)],
        send_sem=hss.at[0], recv_sem=hrs.at[0], device_id={"gz": lax.rem(gz + 1, gzs)}, device_id_type=MESH,
    )
    down = pltpu.make_async_remote_copy(
        src_ref=dup.at[pl.ds(HALO, HALO)], dst_ref=dup.at[pl.ds(BOXES + HALO, HALO)],
        send_sem=hss.at[1], recv_sem=hrs.at[1], device_id={"gz": lax.rem(gz + gzs - 1, gzs)}, device_id_type=MESH,
    )
    up.start()
    down.start()

    own_late = scol[32:64]
    picked2 = jnp.where(own_late < 32, own_late, -1000.0)
    from_own = dot(main_tail_rows(picked2, 32.0, 64), own2[...]) + second_names
    fwd = onehot(fiota((32, 32), 1) == own_late - 32.0).astype(BF16)
    loads[4].wait()
    far_cols = far_ref[...].astype(F32).astype(BF16)
    lanes96 = fiota((BOXES, 96), 1).astype(BF16)
    for l in range(LIST):
        here = jnp.where(lanes96 == far_cols[:, l : l + 1], jnp.ones((), BF16), jnp.zeros((), BF16))
        oh[BOXES * l : BOXES * l + BOXES, :] = here

    base_box = (
        (lax.axis_index("gx") * lax.axis_size("gy") + lax.axis_index("gy")) * gzs + gz
    ) * BOXES - HALO

    def prepare(e):
        tile = dup[e]
        sources[e] = source_rows(tile).astype(BF16)
        charges[e] = jnp.broadcast_to(tile[3:4], (8, 128))

    for e in list(range(HALO, BOXES + HALO)) + [EXT]:
        prepare(e)
    up.wait_recv()
    down.wait_recv()
    for e in list(range(HALO)) + list(range(BOXES + HALO, EXT)):
        prepare(e)
    loads[5].wait()
    loads[6].wait()

    def near_box(g, _):
        lo = iota((8, 128), 1) < SLOTS
        lo48 = iota((48, 128), 1) < SLOTS
        at = pl.ds(pl.multiple_of(g * SLOTS, SLOTS), SLOTS)
        aim = aims[at, :]
        acc = [jnp.zeros((8, 128), F32) for _ in range(8)]
        for p0 in range(0, PAIRS, 2):
            there, weight = [], []
            for p in (p0, p0 + 1):
                if p < PAIRS - 1:
                    first, second = near_ref[2 * p, g], near_ref[2 * p + 1, g]
                    first = jnp.where(first < 0, EXT, jnp.clip(first - base_box, 0, EXT - 1))
                    second = jnp.where(second < 0, EXT, jnp.clip(second - base_box, 0, EXT - 1))
                else:
                    first, second = g + HALO, EXT
                there.append(jnp.where(lo48, sources[first], sources[second]) * factor_ref[p])
                weight.append(jnp.where(lo, charges[first], charges[second]))
            dist = dot(aim, jnp.concatenate(there, axis=1))
            for i in range(2):
                for k in range(8):
                    w = weight[i]
                    if p0 + i == PAIRS - 1:
                        w = jnp.where(iota((8, 128), 1) == 8 * k + iota((8, 128), 0), 0.0, w)
                    acc[k] = acc[k] + w * lax.rsqrt(dist[8 * k : 8 * k + 8, 128 * i : 128 * i + 128])
        accs[at, :] = jnp.concatenate(acc, axis=0)
        return 0

    lax.fori_loop(0, 8, near_box, 0, unroll=8)

    for c in round1:
        c.wait_recv()
    lanes240 = fiota((32, 240), 1)
    from1 = routed(rcv1, 0)
    via = dot(fwd, jnp.broadcast_to(from1, (32, 128)).astype(BF16))[:, 0:1]
    late = jnp.where(jnp.logical_and(own_late >= 32, own_late < 64), via, -1000.0)
    select1 = jnp.concatenate(
        [
            main_tail_rows(late, 8.0, 240),
            onehot(lanes240 == from1).astype(BF16),
            onehot(lanes240 == from1 + 8.0).astype(BF16),
        ],
        axis=0,
    )
    got = dot(select1, rcv1[...].reshape(240, 128))
    is_tail = iota((64, 128), 0) % 16 >= 8
    passed_on = jnp.where(jnp.logical_and(is_tail, iota((64, 128), 1) >= 64), 0.0, got[0:64])
    snd2[...] = (passed_on + from_own).astype(BF16).reshape(4, 16, 128)
    round2 = exchange(1, snd2, rcv2, ss2, rs2)
    held[32:64, 0:128] = got[64:96].astype(BF16)
    held[32:64, 128:256] = got[96:128].astype(BF16)

    lax.fori_loop(8, BOXES, near_box, 0, unroll=8)
    ah, am = split2(accs[...])
    ones = jnp.ones((8, 128), BF16)
    near_row = (dot(ones, ah, NT) + dot(ones, am, NT))[0:1]
    for r in range(BOXES // 2):
        count = jnp.where(lo1, counts_ref[2 * r], counts_ref[2 * r + 1])
        near_out[r : r + 1, :] = jnp.where(slot_in_box < count, near_row[:, 128 * r : 128 * r + 128], 0.0)

    for c in round2:
        c.wait_recv()
    from2 = routed(rcv2, 1)
    select2 = jnp.concatenate(
        [onehot(lanes240 == from2).astype(BF16), onehot(lanes240 == from2 + 8.0).astype(BF16)], axis=0
    )
    got2 = dot(select2, rcv2[...].reshape(240, 128))
    held[64:96, 0:128] = got2[0:32].astype(BF16)
    held[64:96, 128:256] = got2[32:64].astype(BF16)

    table = held[...]

    for first in range(0, LIST, 8):
        count = min(8, LIST - first)
        some = dot(oh[BOXES * first : BOXES * (first + count), :], table).astype(BF16)
        for i in range(count):
            pos = (first + i) * TERMS
            col[:, pos : pos + TERMS] = some[BOXES * i : BOXES * i + BOXES, 0:TERMS]
    op_copy.wait()
    local = dot(opv[...], col[:, 0 : LIST * TERMS], NT)

    l1, l2, l3 = split3(local)
    parts = jnp.concatenate([l1.astype(F32), l2.astype(F32), l3.astype(F32)], axis=1).astype(BF16)
    for blk in range(ATOMS // 256):
        span = slice(256 * blk, 256 * blk + 256)
        boxes = onehot((256 * blk + iota((96, 256), 1)) // SLOTS == iota((96, 256), 0) % BOXES).astype(BF16)
        there = dot(parts, boxes)
        far = jnp.sum(there * tv[0:TERMS, span], axis=0, keepdims=True)
        for h in range(2):
            r = 2 * blk + h
            count = jnp.where(lo1, counts_ref[2 * r], counts_ref[2 * r + 1])
            far_out[r : r + 1, :] = jnp.where(slot_in_box < count, far[:, 128 * h : 128 * h + 128], 0.0)
    for c in round1 + round2 + [up, down]:
        c.wait_send()


def factor_tiles():
    tiles = np.ones((PAIRS, 6, 8, 128), np.float32)
    for p in range(PAIRS):
        for half in range(2):
            shift = SHIFTS[2 * p + half]
            lanes = slice(SLOTS * half, SLOTS * half + SLOTS)
            for c in range(3):
                tiles[p, :, 5 + c, lanes] = shift[c]
            tiles[p, 3, 4, lanes] = sum(c * c for c in shift)
    return tiles.reshape(PAIRS, 48, 128).astype(BF16)


def local_part(leaf_offsets, latent_charges, atom_counts, near_boxes, far_slots, branch_slots, far_operators):
    vmem = pl.BlockSpec(memory_space=pltpu.VMEM)
    hbm = pl.BlockSpec(memory_space=pl.ANY)
    sem = pltpu.SemaphoreType.DMA
    near, far = pl.pallas_call(
        kernel,
        out_shape=[jax.ShapeDtypeStruct((ATOMS // 128, 128), F32)] * 2,
        in_specs=[hbm] * 8,
        out_specs=[vmem, vmem],
        scratch_shapes=[
            pltpu.VMEM((TERMS, LIST * TERMS), BF16),
            pltpu.VMEM((ROWS, ATOMS), F32),
            pltpu.VMEM((8, ATOMS), F32),
            pltpu.VMEM((EXT + 1, 8, 128), F32),
            pltpu.VMEM((ATOMS, 48), BF16),
            pltpu.VMEM((EXT + 1, 48, 128), BF16),
            pltpu.VMEM((EXT + 1, 8, 128), F32),
            pltpu.VMEM((ATOMS, 128), F32),
            pltpu.VMEM((3, ATOMS), F32),
            pltpu.VMEM((1, ATOMS), F32),
            pltpu.SMEM((BOXES,), jnp.int32),
            pltpu.VMEM((1, 8, 8), jnp.int32),
            pltpu.SMEM((len(SHIFTS) - 2, BOXES), jnp.int32),
            pltpu.VMEM((BOXES, LIST), jnp.int32),
            pltpu.VMEM((PAIRS, 48, 128), BF16),
            pltpu.VMEM((64, 128), BF16),
            pltpu.VMEM((4, 16, 128), BF16),
            pltpu.VMEM((4, 16, 128), BF16),
            pltpu.VMEM((GROUP - 1, 16, 128), BF16),
            pltpu.VMEM((GROUP - 1, 16, 128), BF16),
            pltpu.VMEM((96, 256), BF16),
            pltpu.VMEM((LIST * BOXES, 96), BF16),
            pltpu.VMEM((BOXES, 31232), BF16),
            pltpu.VMEM((BOXES, 128), F32),
            sem,
            sem((7,)),
            sem((2,)),
            sem((2,)),
            sem((GROUP - 1,)),
            sem((GROUP - 1,)),
            sem((GROUP - 1,)),
            sem((GROUP - 1,)),
        ],
        compiler_params=pltpu.CompilerParams(
            collective_id=0, has_side_effects=True, vmem_limit_bytes=56 << 20
        ),
    )(
        leaf_offsets,
        latent_charges.reshape(1, ATOMS),
        atom_counts,
        near_boxes,
        far_slots.T,
        branch_slots,
        far_operators,
        factor_tiles(),
    )
    return (near + far).reshape(-1)


def solution(mesh):
    boxes = ("gx", "gy", "gz")
    in_specs = (P(None, boxes), P(boxes), P(boxes), P(None, boxes), P(None, boxes), P(boxes, None, None), P())
    return jax.shard_map(local_part, mesh=mesh, in_specs=in_specs, out_specs=P(boxes), check_vma=False)
```

```python
import itertools

import jax
import jax.numpy as jnp
import numpy as np
from jax import lax
from jax.experimental import pallas as pl
from jax.experimental.pallas import tpu as pltpu
from jax.sharding import PartitionSpec as P

ORDER = 8
TERMS = 165
ROWS = 168
LIST = 189
BOXES = 32
SLOTS = 64
ATOMS = BOXES * SLOTS
HALO = 8
EXT = BOXES + 2 * HALO
SOFT2 = 0.0625
GROUP = 16
F32 = jnp.float32
BF16 = jnp.bfloat16
NT = (((1,), (1,)), ((), ()))
MESH = pl.DeviceIdType.MESH
SHIFTS = [s for s in itertools.product((-1, 0, 1), repeat=3) if s != (0, 0, 0)] + [(0, 0, 0)] * 2
PAIRS = len(SHIFTS) // 2
FARTHEST = (
    (8, 9, 10, 11, 6, 7, 12, 13, 4, 5, 14, 15, 2, 3, 1),
    (10, 6, 14, 9, 11, 2, 8, 5, 7, 13, 15, 1, 3, 4, 12),
)


def degree_start(n):
    return n * (n + 1) * (n + 2) // 6


def low(m):
    return (m & -m).bit_length() - 1


def flips(axis, bits):
    at = lax.axis_index(axis)
    return [(1 << b) * (1 - 2 * lax.rem(lax.div(at, jnp.int32(1 << b)), jnp.int32(2))) for b in range(bits)]


def moved(axis, steps, mask):
    at = lax.axis_index(axis)
    for b, step in enumerate(steps):
        if mask >> b & 1:
            at = at + step
    return at


def iota(shape, dim):
    return lax.broadcasted_iota(jnp.int32, shape, dim)


def fiota(shape, dim):
    return iota(shape, dim).astype(F32)


def split2(v):
    hi = v.astype(BF16)
    return hi, (v - hi.astype(F32)).astype(BF16)


def split3(v):
    hi = v.astype(BF16)
    rest = v - hi.astype(F32)
    mid = rest.astype(BF16)
    return hi, mid, (rest - mid.astype(F32)).astype(BF16)


def dot(a, b, dims=None):
    if dims is None:
        return jnp.dot(a, b, preferred_element_type=F32)
    return lax.dot_general(a, b, dims, preferred_element_type=F32)


def onehot(cond):
    return jnp.where(cond, 1.0, 0.0)


def main_tail_rows(cols, step, width):
    lanes = fiota((8, width), 1)
    rows = []
    for i in range(4):
        at = cols[8 * i : 8 * i + 8]
        rows.append(onehot(lanes == at))
        rows.append(onehot(lanes == at + step))
    return jnp.concatenate(rows, axis=0).astype(BF16)


def routed(got, rnd):
    base = 32.0 * (rnd + 1)
    lane = fiota((1, 128), 1)
    lane8 = (iota((1, 128), 1) % 8).astype(F32)
    sub8 = fiota((8, 1), 0)

    def named(m):
        return got[m - 1].astype(F32)[8:16]

    def as_row(m):
        return pltpu.roll(named(m), 32, 1)[0:1]

    def as_col(m, section):
        at = 64 + 4 * rnd + section
        return named(m)[:, at : at + 1]

    def first_row(m):
        s = as_row(m)
        return jnp.where(s < base, 16.0 * (m - 1) + lane8, 16.0 * m + s - base)

    def first_col(m):
        s = as_col(m, 1)
        return jnp.where(s < base, 16.0 * (m - 1) + sub8, 16.0 * m + s - base)

    def looked_up(m, table_row, section):
        s = as_col(m, section)
        found = jnp.sum(jnp.where(fiota((8, 128), 1) == s - base, table_row, 0.0), axis=1, keepdims=True)
        return jnp.where(s < base, 16.0 * (m - 1) + sub8, found)

    table4 = jnp.where(lane < 8, 16.0 * 4 + lane8, first_row(6))
    s12 = as_row(12)
    at12 = s12 - base
    found12 = jnp.sum(jnp.where(fiota((8, 128), 0) == at12 - 8.0, first_col(14), 0.0), axis=0, keepdims=True)
    found12 = jnp.where(at12 < 8, 16.0 * 12 + at12, found12)
    row12 = jnp.where(at12 < 0, 16.0 * 11 + lane8, found12)
    table8 = jnp.where(lane < 8, 16.0 * 8 + lane8, jnp.where(lane < 16, first_row(10), row12))
    return jnp.concatenate([sub8, first_col(2), looked_up(4, table4, 2), looked_up(8, table8, 3)], axis=0)


def stacked(*cases):
    row = iota((8, 128), 0)
    tiles = [
        jnp.where(row < 3, first, jnp.where(row == 3, third, jnp.where(row == 4, fourth, last)))
        for first, third, fourth, last in cases
    ]
    return jnp.concatenate(tiles, axis=0)


def norm_row(tile):
    square = tile * tile
    return square[0:1] + square[1:2] + square[2:3]


def target_rows(tile):
    row = iota((8, 128), 0)
    both = jnp.where(row == 4, norm_row(tile), jnp.where(row < 3, tile, pltpu.roll(tile, 5, 0)))
    u1, u2, u3 = (part.astype(F32) for part in split3(both))
    return stacked(
        (-2.0 * u1, 1.0, u1, 2.0),
        (-2.0 * u2, 0.0, u2, -2.0 * u1),
        (-2.0 * u3, 0.0, u3, -2.0 * u2),
        (-2.0 * u1, 1.0, 1.0, 2.0),
        (-2.0 * u2, 0.0, 0.0, -2.0 * u3),
        (-2.0 * u1, 1.0, 0.0, 2.0),
    )


def source_rows(tile):
    row = iota((8, 128), 0)
    both = jnp.where(row == 3, norm_row(tile) + SOFT2, jnp.where(row < 3, tile, pltpu.roll(tile, 5, 0)))
    s1, s2, s3 = (part.astype(F32) for part in split3(both))
    return stacked(
        (s1, s1, 1.0, s1),
        (s1, 0.0, 1.0, 1.0),
        (s1, 0.0, 1.0, 1.0),
        (s2, s2, 1.0, s2),
        (s2, 0.0, 0.0, 1.0),
        (s3, s3, 0.0, s3),
    )


def kernel(
    offs_hbm, q_hbm, counts_hbm, near_hbm, far_hbm, branch_hbm, op_hbm, factor_hbm, out_ref,
    opv, tv, p8, dup, aims, sources, charges, accs, offs_ref, q_ref, counts_ref, branch_ref, near_ref, far_ref, factor_ref, own2, snd1, snd2, rcv1, rcv2, held, oh, col, tail,
    op_sem, in_sems, hss, hrs, ss1, rs1, ss2, rs2,
):
    gz = lax.axis_index("gz")
    gzs = lax.axis_size("gz")
    z_flips, y_flips, x_flips = flips("gz", 4), flips("gy", 2), flips("gx", 2)
    at_gz = [{"gz": moved("gz", z_flips, m)} for m in range(GROUP)]
    at_gy = [moved("gy", y_flips, m) for m in range(4)]
    at_gx = [moved("gx", x_flips, m) for m in range(4)]
    partners = (at_gz, [{"gy": at_gy[m & 3], "gx": at_gx[m >> 2]} for m in range(GROUP)])
    barrier = pltpu.get_barrier_semaphore()
    loads = [
        pltpu.make_async_copy(src, dst, in_sems.at[i])
        for i, (src, dst) in enumerate(
            (
                (offs_hbm, offs_ref),
                (q_hbm, q_ref),
                (counts_hbm, counts_ref),
                (branch_hbm, branch_ref),
                (far_hbm, far_ref),
                (near_hbm, near_ref),
                (factor_hbm, factor_ref),
            )
        )
    ]
    for c in loads[:4]:
        c.start()
    for rnd in range(2):
        for m in FARTHEST[rnd]:
            pl.semaphore_signal(barrier, inc=1, device_id=partners[rnd][m], device_id_type=MESH)
    for c in loads[4:]:
        c.start()
    op_copy = pltpu.make_async_copy(op_hbm, opv, op_sem)
    op_copy.start()
    for c in loads[:4]:
        c.wait()

    lo8 = iota((8, 128), 1) < SLOTS
    slot_in_box = iota((1, 128), 1) % SLOTS
    lo1 = iota((1, 128), 1) < SLOTS
    p8[...] = jnp.zeros((8, ATOMS), F32)
    p8[0:3, :] = offs_ref[...]
    for r in range(BOXES // 2):
        count = jnp.where(lo1, counts_ref[2 * r], counts_ref[2 * r + 1])
        span = slice(128 * r, 128 * r + 128)
        p8[3:4, span] = jnp.where(slot_in_box < count, q_ref[:, span], 0.0)
    for r in range(BOXES // 2):
        span = slice(128 * r, 128 * r + 128)
        here = p8[:, span]
        other = pltpu.roll(here, SLOTS, 1)
        dup[HALO + 2 * r] = jnp.where(lo8, here, other)
        dup[HALO + 2 * r + 1] = jnp.where(lo8, other, here)
        aims[span, :] = jnp.transpose(target_rows(here)).astype(BF16)
    dup[EXT] = jnp.zeros((8, 128), F32)

    branch = branch_ref[0].astype(F32).astype(BF16)
    spread = onehot(iota((8, 128), 1) % 8 == iota((8, 128), 0)).astype(BF16)
    wide = dot(branch, spread)
    own_row = jnp.sum(
        jnp.where(iota((8, 128), 1) // 8 == iota((8, 128), 0), wide, 0.0), axis=0, keepdims=True
    )
    stretch = onehot(iota((64, 8), 0) // 8 == iota((64, 8), 1)).astype(BF16)
    tall = dot(stretch, branch)
    scol = jnp.sum(jnp.where(iota((64, 8), 1) == iota((64, 8), 0) % 8, tall, 0.0), axis=1, keepdims=True)

    def named_tile(rnd):
        lanes = iota((8, 128), 1)
        tile = jnp.where(lanes >= 96, pltpu.roll(jnp.broadcast_to(own_row, (8, 128)), 96 - 32 * rnd, 1), 0.0)
        for i in range(4 * rnd, 4 * rnd + 4):
            tile = jnp.where(lanes == 64 + i, scol[8 * i : 8 * i + 8], tile)
        none = jnp.zeros((8, 128), F32)
        return jnp.concatenate([none, tile] * 4, axis=0)

    def terms_block(blk, _):
        span = pl.ds(pl.multiple_of(blk * 256, 256), 256)
        x, y, z = (2.0 * p8[c : c + 1, span] for c in range(3))
        tv[0:1, span] = jnp.ones((1, 256), F32)
        for n in range(1, ORDER + 1):
            before, here, kept = degree_start(n - 1), degree_start(n), n * (n + 1) // 2
            tv[here : here + kept, span] = tv[before : before + kept, span] * x
            tv[here + kept : here + kept + n, span] = tv[before + kept - n : before + kept, span] * y
            tv[here + kept + n : here + kept + n + 1, span] = tv[before + kept - 1 : before + kept, span] * z
        tv[TERMS:ROWS, span] = jnp.zeros((ROWS - TERMS, 256), F32)
        return 0

    lax.fori_loop(0, ATOMS // 256, terms_block, 0)

    head = jnp.zeros((64, ROWS), F32)
    rest = jnp.zeros((32, ROWS), F32)
    for blk in range(ATOMS // 256):
        span = slice(256 * blk, 256 * blk + 256)
        mine = (256 * blk + iota((BOXES, 256), 1)) // SLOTS == iota((BOXES, 256), 0)
        qh, qm = split2(jnp.where(mine, p8[3:4, span], 0.0))
        th, tm = split2(tv[:, span])
        head = head + dot(jnp.concatenate([qh, qm], axis=0), th, NT)
        rest = rest + dot(qh, tm, NT)
    multipoles = head[:32] + head[32:] + rest
    tail[...] = jnp.zeros((32, 128), F32)
    tail[:, 0 : ROWS - 128] = multipoles[:, 128:ROWS]
    own_main = multipoles[:, 0:128].astype(BF16)
    own_tail = tail[...].astype(BF16)
    own2[0:32] = own_main
    own2[32:64] = own_tail
    held[0:32, 0:128] = own_main
    held[0:32, 128:256] = own_tail

    picked1 = jnp.where(scol[:32] < 32, scol[:32], -1000.0)
    first_payload = dot(main_tail_rows(picked1, 32.0, 64), own2[...]) + named_tile(0)
    snd1[...] = first_payload.astype(BF16).reshape(4, 16, 128)
    second_names = named_tile(1)

    def exchange(rnd, snd, rcv, ss, rs):
        out = []
        for m in FARTHEST[rnd]:
            c = pltpu.make_async_remote_copy(
                src_ref=snd.at[low(m)], dst_ref=rcv.at[m - 1], send_sem=ss.at[m - 1], recv_sem=rs.at[m - 1],
                device_id=partners[rnd][m], device_id_type=MESH,
            )
            c.start()
            out.append(c)
        return out

    pl.semaphore_wait(barrier, 2 * (GROUP - 1))
    round1 = exchange(0, snd1, rcv1, ss1, rs1)
    up = pltpu.make_async_remote_copy(
        src_ref=dup.at[pl.ds(BOXES, HALO)], dst_ref=dup.at[pl.ds(0, HALO)],
        send_sem=hss.at[0], recv_sem=hrs.at[0], device_id={"gz": lax.rem(gz + 1, gzs)}, device_id_type=MESH,
    )
    down = pltpu.make_async_remote_copy(
        src_ref=dup.at[pl.ds(HALO, HALO)], dst_ref=dup.at[pl.ds(BOXES + HALO, HALO)],
        send_sem=hss.at[1], recv_sem=hrs.at[1], device_id={"gz": lax.rem(gz + gzs - 1, gzs)}, device_id_type=MESH,
    )
    up.start()
    down.start()

    own_late = scol[32:64]
    picked2 = jnp.where(own_late < 32, own_late, -1000.0)
    from_own = dot(main_tail_rows(picked2, 32.0, 64), own2[...]) + second_names
    fwd = onehot(fiota((32, 32), 1) == own_late - 32.0).astype(BF16)
    loads[4].wait()
    far_cols = far_ref[...].astype(F32).astype(BF16)
    lanes96 = fiota((BOXES, 96), 1).astype(BF16)
    for l in range(LIST):
        here = jnp.where(lanes96 == far_cols[:, l : l + 1], jnp.ones((), BF16), jnp.zeros((), BF16))
        oh[BOXES * l : BOXES * l + BOXES, :] = here

    base_box = (
        (lax.axis_index("gx") * lax.axis_size("gy") + lax.axis_index("gy")) * gzs + gz
    ) * BOXES - HALO

    def prepare(e):
        tile = dup[e]
        sources[e] = source_rows(tile).astype(BF16)
        charges[e] = jnp.broadcast_to(tile[3:4], (8, 128))

    for e in list(range(HALO, BOXES + HALO)) + [EXT]:
        prepare(e)
    up.wait_recv()
    down.wait_recv()
    for e in list(range(HALO)) + list(range(BOXES + HALO, EXT)):
        prepare(e)
    loads[5].wait()
    loads[6].wait()

    def near_box(g, _):
        lo = iota((8, 128), 1) < SLOTS
        lo48 = iota((48, 128), 1) < SLOTS
        at = pl.ds(pl.multiple_of(g * SLOTS, SLOTS), SLOTS)
        aim = aims[at, :]
        acc = [jnp.zeros((8, 128), F32) for _ in range(8)]
        for p0 in range(0, PAIRS, 2):
            there, weight = [], []
            for p in (p0, p0 + 1):
                if p < PAIRS - 1:
                    first, second = near_ref[2 * p, g], near_ref[2 * p + 1, g]
                    first = jnp.where(first < 0, EXT, jnp.clip(first - base_box, 0, EXT - 1))
                    second = jnp.where(second < 0, EXT, jnp.clip(second - base_box, 0, EXT - 1))
                else:
                    first, second = g + HALO, EXT
                there.append(jnp.where(lo48, sources[first], sources[second]) * factor_ref[p])
                weight.append(jnp.where(lo, charges[first], charges[second]))
            dist = dot(aim, jnp.concatenate(there, axis=1))
            for i in range(2):
                for k in range(8):
                    w = weight[i]
                    if p0 + i == PAIRS - 1:
                        w = jnp.where(iota((8, 128), 1) == 8 * k + iota((8, 128), 0), 0.0, w)
                    acc[k] = acc[k] + w * lax.rsqrt(dist[8 * k : 8 * k + 8, 128 * i : 128 * i + 128])
        accs[at, :] = jnp.concatenate(acc, axis=0)
        return 0

    lax.fori_loop(0, 8, near_box, 0, unroll=8)

    for c in round1:
        c.wait_recv()
    lanes240 = fiota((32, 240), 1)
    from1 = routed(rcv1, 0)
    via = dot(fwd, jnp.broadcast_to(from1, (32, 128)).astype(BF16))[:, 0:1]
    late = jnp.where(jnp.logical_and(own_late >= 32, own_late < 64), via, -1000.0)
    select1 = jnp.concatenate(
        [
            main_tail_rows(late, 8.0, 240),
            onehot(lanes240 == from1).astype(BF16),
            onehot(lanes240 == from1 + 8.0).astype(BF16),
        ],
        axis=0,
    )
    got = dot(select1, rcv1[...].reshape(240, 128))
    is_tail = iota((64, 128), 0) % 16 >= 8
    passed_on = jnp.where(jnp.logical_and(is_tail, iota((64, 128), 1) >= 64), 0.0, got[0:64])
    snd2[...] = (passed_on + from_own).astype(BF16).reshape(4, 16, 128)
    round2 = exchange(1, snd2, rcv2, ss2, rs2)
    held[32:64, 0:128] = got[64:96].astype(BF16)
    held[32:64, 128:256] = got[96:128].astype(BF16)

    lax.fori_loop(8, BOXES, near_box, 0, unroll=8)
    ah, am = split2(accs[...])
    ones = jnp.ones((8, 128), BF16)
    near_row = (dot(ones, ah, NT) + dot(ones, am, NT))[0:1]
    for r in range(BOXES // 2):
        count = jnp.where(lo1, counts_ref[2 * r], counts_ref[2 * r + 1])
        out_ref[r : r + 1, :] = jnp.where(slot_in_box < count, near_row[:, 128 * r : 128 * r + 128], 0.0)

    for c in round2:
        c.wait_recv()
    from2 = routed(rcv2, 1)
    select2 = jnp.concatenate(
        [onehot(lanes240 == from2).astype(BF16), onehot(lanes240 == from2 + 8.0).astype(BF16)], axis=0
    )
    got2 = dot(select2, rcv2[...].reshape(240, 128))
    held[64:96, 0:128] = got2[0:32].astype(BF16)
    held[64:96, 128:256] = got2[32:64].astype(BF16)

    table = held[...]

    for first in range(0, LIST, 8):
        count = min(8, LIST - first)
        some = dot(oh[BOXES * first : BOXES * (first + count), :], table).astype(BF16)
        for i in range(count):
            pos = (first + i) * TERMS
            col[:, pos : pos + TERMS] = some[BOXES * i : BOXES * i + BOXES, 0:TERMS]
    op_copy.wait()
    local = dot(opv[...], col[:, 0 : LIST * TERMS], NT)

    l1, l2, l3 = split3(local)
    parts = jnp.concatenate([l1.astype(F32), l2.astype(F32), l3.astype(F32)], axis=1).astype(BF16)
    for blk in range(ATOMS // 256):
        span = slice(256 * blk, 256 * blk + 256)
        boxes = onehot((256 * blk + iota((96, 256), 1)) // SLOTS == iota((96, 256), 0) % BOXES).astype(BF16)
        there = dot(parts, boxes)
        far = jnp.sum(there * tv[0:TERMS, span], axis=0, keepdims=True)
        for h in range(2):
            r = 2 * blk + h
            count = jnp.where(lo1, counts_ref[2 * r], counts_ref[2 * r + 1])
            here = jnp.where(slot_in_box < count, far[:, 128 * h : 128 * h + 128], 0.0)
            out_ref[r : r + 1, :] = out_ref[r : r + 1, :] + here
    for c in round1 + round2 + [up, down]:
        c.wait_send()


def factor_tiles():
    tiles = np.ones((PAIRS, 6, 8, 128), np.float32)
    for p in range(PAIRS):
        for half in range(2):
            shift = SHIFTS[2 * p + half]
            lanes = slice(SLOTS * half, SLOTS * half + SLOTS)
            for c in range(3):
                tiles[p, :, 5 + c, lanes] = shift[c]
            tiles[p, 3, 4, lanes] = sum(c * c for c in shift)
    return tiles.reshape(PAIRS, 48, 128).astype(BF16)


def local_part(leaf_offsets, latent_charges, atom_counts, near_boxes, far_slots, branch_slots, far_operators):
    vmem = pl.BlockSpec(memory_space=pltpu.VMEM)
    hbm = pl.BlockSpec(memory_space=pl.ANY)
    sem = pltpu.SemaphoreType.DMA
    out = pl.pallas_call(
        kernel,
        out_shape=jax.ShapeDtypeStruct((ATOMS // 128, 128), F32),
        in_specs=[hbm] * 8,
        out_specs=vmem,
        scratch_shapes=[
            pltpu.VMEM((TERMS, LIST * TERMS), BF16),
            pltpu.VMEM((ROWS, ATOMS), F32),
            pltpu.VMEM((8, ATOMS), F32),
            pltpu.VMEM((EXT + 1, 8, 128), F32),
            pltpu.VMEM((ATOMS, 48), BF16),
            pltpu.VMEM((EXT + 1, 48, 128), BF16),
            pltpu.VMEM((EXT + 1, 8, 128), F32),
            pltpu.VMEM((ATOMS, 128), F32),
            pltpu.VMEM((3, ATOMS), F32),
            pltpu.VMEM((1, ATOMS), F32),
            pltpu.SMEM((BOXES,), jnp.int32),
            pltpu.VMEM((1, 8, 8), jnp.int32),
            pltpu.SMEM((len(SHIFTS) - 2, BOXES), jnp.int32),
            pltpu.VMEM((BOXES, LIST), jnp.int32),
            pltpu.VMEM((PAIRS, 48, 128), BF16),
            pltpu.VMEM((64, 128), BF16),
            pltpu.VMEM((4, 16, 128), BF16),
            pltpu.VMEM((4, 16, 128), BF16),
            pltpu.VMEM((GROUP - 1, 16, 128), BF16),
            pltpu.VMEM((GROUP - 1, 16, 128), BF16),
            pltpu.VMEM((96, 256), BF16),
            pltpu.VMEM((LIST * BOXES, 96), BF16),
            pltpu.VMEM((BOXES, 31232), BF16),
            pltpu.VMEM((BOXES, 128), F32),
            sem,
            sem((7,)),
            sem((2,)),
            sem((2,)),
            sem((GROUP - 1,)),
            sem((GROUP - 1,)),
            sem((GROUP - 1,)),
            sem((GROUP - 1,)),
        ],
        compiler_params=pltpu.CompilerParams(
            collective_id=0, has_side_effects=True, vmem_limit_bytes=56 << 20
        ),
    )(
        leaf_offsets,
        latent_charges.reshape(1, ATOMS),
        atom_counts,
        near_boxes,
        far_slots.T,
        branch_slots,
        far_operators,
        factor_tiles(),
    )
    return out.reshape(-1)


def solution(mesh):
    boxes = ("gx", "gy", "gz")
    in_specs = (P(None, boxes), P(boxes), P(boxes), P(None, boxes), P(None, boxes), P(boxes, None, None), P())
    return jax.shard_map(local_part, mesh=mesh, in_specs=in_specs, out_specs=P(boxes), check_vma=False)
```

```python
import itertools

import jax
import jax.numpy as jnp
import numpy as np
from jax import lax
from jax.experimental import pallas as pl
from jax.experimental.pallas import tpu as pltpu
from jax.sharding import PartitionSpec as P

ORDER = 8
TERMS = 165
ROWS = 168
LIST = 189
BOXES = 32
SLOTS = 64
ATOMS = BOXES * SLOTS
HALO = 8
EXT = BOXES + 2 * HALO
SOFT2 = 0.0625
GROUP = 16
F32 = jnp.float32
BF16 = jnp.bfloat16
NT = (((1,), (1,)), ((), ()))
MESH = pl.DeviceIdType.MESH
SHIFTS = [s for s in itertools.product((-1, 0, 1), repeat=3) if s != (0, 0, 0)] + [(0, 0, 0)] * 2
PAIRS = len(SHIFTS) // 2
FARTHEST = (
    (8, 9, 10, 11, 6, 7, 12, 13, 4, 5, 14, 15, 2, 3, 1),
    (10, 6, 14, 9, 11, 2, 8, 5, 7, 13, 15, 1, 3, 4, 12),
)


def degree_start(n):
    return n * (n + 1) * (n + 2) // 6


def low(m):
    return (m & -m).bit_length() - 1


def flips(axis, bits):
    at = lax.axis_index(axis)
    return [(1 << b) * (1 - 2 * lax.rem(lax.div(at, jnp.int32(1 << b)), jnp.int32(2))) for b in range(bits)]


def moved(axis, steps, mask):
    at = lax.axis_index(axis)
    for b, step in enumerate(steps):
        if mask >> b & 1:
            at = at + step
    return at


def iota(shape, dim):
    return lax.broadcasted_iota(jnp.int32, shape, dim)


def fiota(shape, dim):
    return iota(shape, dim).astype(F32)


def split2(v):
    hi = v.astype(BF16)
    return hi, (v - hi.astype(F32)).astype(BF16)


def split3(v):
    hi = v.astype(BF16)
    rest = v - hi.astype(F32)
    mid = rest.astype(BF16)
    return hi, mid, (rest - mid.astype(F32)).astype(BF16)


def dot(a, b, dims=None):
    if dims is None:
        return jnp.dot(a, b, preferred_element_type=F32)
    return lax.dot_general(a, b, dims, preferred_element_type=F32)


def onehot(cond):
    return jnp.where(cond, 1.0, 0.0)


def main_tail_rows(cols, step, width):
    lanes = fiota((8, width), 1)
    rows = []
    for i in range(4):
        at = cols[8 * i : 8 * i + 8]
        rows.append(onehot(lanes == at))
        rows.append(onehot(lanes == at + step))
    return jnp.concatenate(rows, axis=0).astype(BF16)


def routed(got, rnd):
    base = 32.0 * (rnd + 1)
    lane = fiota((1, 128), 1)
    lane8 = (iota((1, 128), 1) % 8).astype(F32)
    sub8 = fiota((8, 1), 0)

    def named(m):
        return got[m - 1].astype(F32)[8:16]

    def as_row(m):
        return pltpu.roll(named(m), 32, 1)[0:1]

    def as_col(m, section):
        at = 64 + 4 * rnd + section
        return named(m)[:, at : at + 1]

    def first_row(m):
        s = as_row(m)
        return jnp.where(s < base, 16.0 * (m - 1) + lane8, 16.0 * m + s - base)

    def first_col(m):
        s = as_col(m, 1)
        return jnp.where(s < base, 16.0 * (m - 1) + sub8, 16.0 * m + s - base)

    def looked_up(m, table_row, section):
        s = as_col(m, section)
        found = jnp.sum(jnp.where(fiota((8, 128), 1) == s - base, table_row, 0.0), axis=1, keepdims=True)
        return jnp.where(s < base, 16.0 * (m - 1) + sub8, found)

    table4 = jnp.where(lane < 8, 16.0 * 4 + lane8, first_row(6))
    s12 = as_row(12)
    at12 = s12 - base
    found12 = jnp.sum(jnp.where(fiota((8, 128), 0) == at12 - 8.0, first_col(14), 0.0), axis=0, keepdims=True)
    found12 = jnp.where(at12 < 8, 16.0 * 12 + at12, found12)
    row12 = jnp.where(at12 < 0, 16.0 * 11 + lane8, found12)
    table8 = jnp.where(lane < 8, 16.0 * 8 + lane8, jnp.where(lane < 16, first_row(10), row12))
    return jnp.concatenate([sub8, first_col(2), looked_up(4, table4, 2), looked_up(8, table8, 3)], axis=0)


def stacked(*cases):
    row = iota((8, 128), 0)
    tiles = [
        jnp.where(row < 3, first, jnp.where(row == 3, third, jnp.where(row == 4, fourth, last)))
        for first, third, fourth, last in cases
    ]
    return jnp.concatenate(tiles, axis=0)


def norm_row(tile):
    square = tile * tile
    return square[0:1] + square[1:2] + square[2:3]


def target_rows(tile):
    row = iota((8, 128), 0)
    both = jnp.where(row == 4, norm_row(tile), jnp.where(row < 3, tile, pltpu.roll(tile, 5, 0)))
    u1, u2, u3 = (part.astype(F32) for part in split3(both))
    return stacked(
        (-2.0 * u1, 1.0, u1, 2.0),
        (-2.0 * u2, 0.0, u2, -2.0 * u1),
        (-2.0 * u3, 0.0, u3, -2.0 * u2),
        (-2.0 * u1, 1.0, 1.0, 2.0),
        (-2.0 * u2, 0.0, 0.0, -2.0 * u3),
        (-2.0 * u1, 1.0, 0.0, 2.0),
    )


def source_rows(tile):
    row = iota((8, 128), 0)
    both = jnp.where(row == 3, norm_row(tile) + SOFT2, jnp.where(row < 3, tile, pltpu.roll(tile, 5, 0)))
    s1, s2, s3 = (part.astype(F32) for part in split3(both))
    return stacked(
        (s1, s1, 1.0, s1),
        (s1, 0.0, 1.0, 1.0),
        (s1, 0.0, 1.0, 1.0),
        (s2, s2, 1.0, s2),
        (s2, 0.0, 0.0, 1.0),
        (s3, s3, 0.0, s3),
    )


def kernel(
    offs_hbm, q_hbm, counts_hbm, near_hbm, far_hbm, branch_hbm, op_hbm, factor_hbm, near_out, far_out,
    opv, tv, p8, dup, aims, sources, charges, accs, offs_ref, q_ref, counts_ref, branch_ref, near_ref, far_ref, factor_ref, own2, snd1, snd2, rcv1, rcv2, held, oh, col, tail,
    op_sem, in_sems, hss, hrs, ss1, rs1, ss2, rs2,
):
    gz = lax.axis_index("gz")
    gzs = lax.axis_size("gz")
    z_flips, y_flips, x_flips = flips("gz", 4), flips("gy", 2), flips("gx", 2)
    at_gz = [{"gz": moved("gz", z_flips, m)} for m in range(GROUP)]
    at_gy = [moved("gy", y_flips, m) for m in range(4)]
    at_gx = [moved("gx", x_flips, m) for m in range(4)]
    partners = (at_gz, [{"gy": at_gy[m & 3], "gx": at_gx[m >> 2]} for m in range(GROUP)])
    barrier = pltpu.get_barrier_semaphore()
    loads = [
        pltpu.make_async_copy(src, dst, in_sems.at[i])
        for i, (src, dst) in enumerate(
            (
                (offs_hbm, offs_ref),
                (q_hbm, q_ref),
                (counts_hbm, counts_ref),
                (branch_hbm, branch_ref),
                (far_hbm, far_ref),
                (near_hbm, near_ref),
                (factor_hbm, factor_ref),
            )
        )
    ]
    for c in loads[:4]:
        c.start()
    for rnd in range(2):
        for m in FARTHEST[rnd]:
            pl.semaphore_signal(barrier, inc=1, device_id=partners[rnd][m], device_id_type=MESH)
    for c in loads[4:]:
        c.start()
    op_copy = pltpu.make_async_copy(op_hbm, opv, op_sem)
    op_copy.start()
    for c in loads[:4]:
        c.wait()

    lo8 = iota((8, 128), 1) < SLOTS
    slot_in_box = iota((1, 128), 1) % SLOTS
    lo1 = iota((1, 128), 1) < SLOTS
    p8[...] = jnp.zeros((8, ATOMS), F32)
    p8[0:3, :] = offs_ref[...]
    for r in range(BOXES // 2):
        count = jnp.where(lo1, counts_ref[2 * r], counts_ref[2 * r + 1])
        span = slice(128 * r, 128 * r + 128)
        p8[3:4, span] = jnp.where(slot_in_box < count, q_ref[:, span], 0.0)
    for r in range(BOXES // 2):
        span = slice(128 * r, 128 * r + 128)
        here = p8[:, span]
        other = pltpu.roll(here, SLOTS, 1)
        dup[HALO + 2 * r] = jnp.where(lo8, here, other)
        dup[HALO + 2 * r + 1] = jnp.where(lo8, other, here)
        aims[span, :] = jnp.transpose(target_rows(here)).astype(BF16)
    dup[EXT] = jnp.zeros((8, 128), F32)

    branch = branch_ref[0].astype(F32).astype(BF16)
    spread = onehot(iota((8, 128), 1) % 8 == iota((8, 128), 0)).astype(BF16)
    wide = dot(branch, spread)
    own_row = jnp.sum(
        jnp.where(iota((8, 128), 1) // 8 == iota((8, 128), 0), wide, 0.0), axis=0, keepdims=True
    )
    stretch = onehot(iota((64, 8), 0) // 8 == iota((64, 8), 1)).astype(BF16)
    tall = dot(stretch, branch)
    scol = jnp.sum(jnp.where(iota((64, 8), 1) == iota((64, 8), 0) % 8, tall, 0.0), axis=1, keepdims=True)

    def named_tile(rnd):
        lanes = iota((8, 128), 1)
        tile = jnp.where(lanes >= 96, pltpu.roll(jnp.broadcast_to(own_row, (8, 128)), 96 - 32 * rnd, 1), 0.0)
        for i in range(4 * rnd, 4 * rnd + 4):
            tile = jnp.where(lanes == 64 + i, scol[8 * i : 8 * i + 8], tile)
        none = jnp.zeros((8, 128), F32)
        return jnp.concatenate([none, tile] * 4, axis=0)

    def terms_block(blk, _):
        span = pl.ds(pl.multiple_of(blk * 256, 256), 256)
        x, y, z = (2.0 * p8[c : c + 1, span] for c in range(3))
        tv[0:1, span] = jnp.ones((1, 256), F32)
        for n in range(1, ORDER + 1):
            before, here, kept = degree_start(n - 1), degree_start(n), n * (n + 1) // 2
            tv[here : here + kept, span] = tv[before : before + kept, span] * x
            tv[here + kept : here + kept + n, span] = tv[before + kept - n : before + kept, span] * y
            tv[here + kept + n : here + kept + n + 1, span] = tv[before + kept - 1 : before + kept, span] * z
        tv[TERMS:ROWS, span] = jnp.zeros((ROWS - TERMS, 256), F32)
        return 0

    lax.fori_loop(0, ATOMS // 256, terms_block, 0, unroll=4)

    head = jnp.zeros((64, ROWS), F32)
    rest = jnp.zeros((32, ROWS), F32)
    for blk in range(ATOMS // 256):
        span = slice(256 * blk, 256 * blk + 256)
        mine = (256 * blk + iota((BOXES, 256), 1)) // SLOTS == iota((BOXES, 256), 0)
        qh, qm = split2(jnp.where(mine, p8[3:4, span], 0.0))
        th, tm = split2(tv[:, span])
        head = head + dot(jnp.concatenate([qh, qm], axis=0), th, NT)
        rest = rest + dot(qh, tm, NT)
    multipoles = head[:32] + head[32:] + rest
    tail[...] = jnp.zeros((32, 128), F32)
    tail[:, 0 : ROWS - 128] = multipoles[:, 128:ROWS]
    own_main = multipoles[:, 0:128].astype(BF16)
    own_tail = tail[...].astype(BF16)
    own2[0:32] = own_main
    own2[32:64] = own_tail
    held[0:32, 0:128] = own_main
    held[0:32, 128:256] = own_tail

    picked1 = jnp.where(scol[:32] < 32, scol[:32], -1000.0)
    first_payload = dot(main_tail_rows(picked1, 32.0, 64), own2[...]) + named_tile(0)
    snd1[...] = first_payload.astype(BF16).reshape(4, 16, 128)
    second_names = named_tile(1)

    def exchange(rnd, snd, rcv, ss, rs):
        out = []
        for m in FARTHEST[rnd]:
            c = pltpu.make_async_remote_copy(
                src_ref=snd.at[low(m)], dst_ref=rcv.at[m - 1], send_sem=ss.at[m - 1], recv_sem=rs.at[m - 1],
                device_id=partners[rnd][m], device_id_type=MESH,
            )
            c.start()
            out.append(c)
        return out

    pl.semaphore_wait(barrier, 2 * (GROUP - 1))
    round1 = exchange(0, snd1, rcv1, ss1, rs1)
    up = pltpu.make_async_remote_copy(
        src_ref=dup.at[pl.ds(BOXES, HALO)], dst_ref=dup.at[pl.ds(0, HALO)],
        send_sem=hss.at[0], recv_sem=hrs.at[0], device_id={"gz": lax.rem(gz + 1, gzs)}, device_id_type=MESH,
    )
    down = pltpu.make_async_remote_copy(
        src_ref=dup.at[pl.ds(HALO, HALO)], dst_ref=dup.at[pl.ds(BOXES + HALO, HALO)],
        send_sem=hss.at[1], recv_sem=hrs.at[1], device_id={"gz": lax.rem(gz + gzs - 1, gzs)}, device_id_type=MESH,
    )
    up.start()
    down.start()

    own_late = scol[32:64]
    picked2 = jnp.where(own_late < 32, own_late, -1000.0)
    from_own = dot(main_tail_rows(picked2, 32.0, 64), own2[...]) + second_names
    fwd = onehot(fiota((32, 32), 1) == own_late - 32.0).astype(BF16)
    loads[4].wait()
    far_cols = far_ref[...].astype(F32).astype(BF16)
    lanes96 = fiota((BOXES, 96), 1).astype(BF16)
    for l in range(LIST):
        here = jnp.where(lanes96 == far_cols[:, l : l + 1], jnp.ones((), BF16), jnp.zeros((), BF16))
        oh[BOXES * l : BOXES * l + BOXES, :] = here

    base_box = (
        (lax.axis_index("gx") * lax.axis_size("gy") + lax.axis_index("gy")) * gzs + gz
    ) * BOXES - HALO

    def prepare(e):
        tile = dup[e]
        sources[e] = source_rows(tile).astype(BF16)
        charges[e] = jnp.broadcast_to(tile[3:4], (8, 128))

    for e in list(range(HALO, BOXES + HALO)) + [EXT]:
        prepare(e)
    up.wait_recv()
    down.wait_recv()
    for e in list(range(HALO)) + list(range(BOXES + HALO, EXT)):
        prepare(e)
    loads[5].wait()
    loads[6].wait()

    def near_box(g, _):
        lo = iota((8, 128), 1) < SLOTS
        lo48 = iota((48, 128), 1) < SLOTS
        at = pl.ds(pl.multiple_of(g * SLOTS, SLOTS), SLOTS)
        aim = aims[at, :]
        acc = [jnp.zeros((8, 128), F32) for _ in range(8)]
        for p0 in range(0, PAIRS, 2):
            there, weight = [], []
            for p in (p0, p0 + 1):
                if p < PAIRS - 1:
                    first, second = near_ref[2 * p, g], near_ref[2 * p + 1, g]
                    first = jnp.where(first < 0, EXT, jnp.clip(first - base_box, 0, EXT - 1))
                    second = jnp.where(second < 0, EXT, jnp.clip(second - base_box, 0, EXT - 1))
                else:
                    first, second = g + HALO, EXT
                there.append(jnp.where(lo48, sources[first], sources[second]) * factor_ref[p])
                weight.append(jnp.where(lo, charges[first], charges[second]))
            dist = dot(aim, jnp.concatenate(there, axis=1))
            for i in range(2):
                for k in range(8):
                    w = weight[i]
                    if p0 + i == PAIRS - 1:
                        w = jnp.where(iota((8, 128), 1) == 8 * k + iota((8, 128), 0), 0.0, w)
                    acc[k] = acc[k] + w * lax.rsqrt(dist[8 * k : 8 * k + 8, 128 * i : 128 * i + 128])
        accs[at, :] = jnp.concatenate(acc, axis=0)
        return 0

    lax.fori_loop(0, 8, near_box, 0, unroll=8)

    for c in round1:
        c.wait_recv()
    lanes240 = fiota((32, 240), 1)
    from1 = routed(rcv1, 0)
    via = dot(fwd, jnp.broadcast_to(from1, (32, 128)).astype(BF16))[:, 0:1]
    late = jnp.where(jnp.logical_and(own_late >= 32, own_late < 64), via, -1000.0)
    select1 = jnp.concatenate(
        [
            main_tail_rows(late, 8.0, 240),
            onehot(lanes240 == from1).astype(BF16),
            onehot(lanes240 == from1 + 8.0).astype(BF16),
        ],
        axis=0,
    )
    got = dot(select1, rcv1[...].reshape(240, 128))
    is_tail = iota((64, 128), 0) % 16 >= 8
    passed_on = jnp.where(jnp.logical_and(is_tail, iota((64, 128), 1) >= 64), 0.0, got[0:64])
    snd2[...] = (passed_on + from_own).astype(BF16).reshape(4, 16, 128)
    round2 = exchange(1, snd2, rcv2, ss2, rs2)
    held[32:64, 0:128] = got[64:96].astype(BF16)
    held[32:64, 128:256] = got[96:128].astype(BF16)

    lax.fori_loop(8, BOXES, near_box, 0, unroll=12)
    ah, am = split2(accs[...])
    ones = jnp.ones((8, 128), BF16)
    near_row = (dot(ones, ah, NT) + dot(ones, am, NT))[0:1]
    for r in range(BOXES // 2):
        count = jnp.where(lo1, counts_ref[2 * r], counts_ref[2 * r + 1])
        near_out[r : r + 1, :] = jnp.where(slot_in_box < count, near_row[:, 128 * r : 128 * r + 128], 0.0)

    for c in round2:
        c.wait_recv()
    from2 = routed(rcv2, 1)
    select2 = jnp.concatenate(
        [onehot(lanes240 == from2).astype(BF16), onehot(lanes240 == from2 + 8.0).astype(BF16)], axis=0
    )
    got2 = dot(select2, rcv2[...].reshape(240, 128))
    held[64:96, 0:128] = got2[0:32].astype(BF16)
    held[64:96, 128:256] = got2[32:64].astype(BF16)

    table = held[...]

    for first in range(0, LIST, 8):
        count = min(8, LIST - first)
        some = dot(oh[BOXES * first : BOXES * (first + count), :], table).astype(BF16)
        for i in range(count):
            pos = (first + i) * TERMS
            col[:, pos : pos + TERMS] = some[BOXES * i : BOXES * i + BOXES, 0:TERMS]
    op_copy.wait()
    local = dot(opv[...], col[:, 0 : LIST * TERMS], NT)

    l1, l2, l3 = split3(local)
    parts = jnp.concatenate([l1.astype(F32), l2.astype(F32), l3.astype(F32)], axis=1).astype(BF16)
    for blk in range(ATOMS // 256):
        span = slice(256 * blk, 256 * blk + 256)
        boxes = onehot((256 * blk + iota((96, 256), 1)) // SLOTS == iota((96, 256), 0) % BOXES).astype(BF16)
        there = dot(parts, boxes)
        far = jnp.sum(there * tv[0:TERMS, span], axis=0, keepdims=True)
        for h in range(2):
            r = 2 * blk + h
            count = jnp.where(lo1, counts_ref[2 * r], counts_ref[2 * r + 1])
            far_out[r : r + 1, :] = jnp.where(slot_in_box < count, far[:, 128 * h : 128 * h + 128], 0.0)
    for c in round1 + round2 + [up, down]:
        c.wait_send()


def factor_tiles():
    tiles = np.ones((PAIRS, 6, 8, 128), np.float32)
    for p in range(PAIRS):
        for half in range(2):
            shift = SHIFTS[2 * p + half]
            lanes = slice(SLOTS * half, SLOTS * half + SLOTS)
            for c in range(3):
                tiles[p, :, 5 + c, lanes] = shift[c]
            tiles[p, 3, 4, lanes] = sum(c * c for c in shift)
    return tiles.reshape(PAIRS, 48, 128).astype(BF16)


def local_part(leaf_offsets, latent_charges, atom_counts, near_boxes, far_slots, branch_slots, far_operators):
    vmem = pl.BlockSpec(memory_space=pltpu.VMEM)
    hbm = pl.BlockSpec(memory_space=pl.ANY)
    sem = pltpu.SemaphoreType.DMA
    near, far = pl.pallas_call(
        kernel,
        out_shape=[jax.ShapeDtypeStruct((ATOMS // 128, 128), F32)] * 2,
        in_specs=[hbm] * 8,
        out_specs=[vmem, vmem],
        scratch_shapes=[
            pltpu.VMEM((TERMS, LIST * TERMS), BF16),
            pltpu.VMEM((ROWS, ATOMS), F32),
            pltpu.VMEM((8, ATOMS), F32),
            pltpu.VMEM((EXT + 1, 8, 128), F32),
            pltpu.VMEM((ATOMS, 48), BF16),
            pltpu.VMEM((EXT + 1, 48, 128), BF16),
            pltpu.VMEM((EXT + 1, 8, 128), F32),
            pltpu.VMEM((ATOMS, 128), F32),
            pltpu.VMEM((3, ATOMS), F32),
            pltpu.VMEM((1, ATOMS), F32),
            pltpu.SMEM((BOXES,), jnp.int32),
            pltpu.VMEM((1, 8, 8), jnp.int32),
            pltpu.SMEM((len(SHIFTS) - 2, BOXES), jnp.int32),
            pltpu.VMEM((BOXES, LIST), jnp.int32),
            pltpu.VMEM((PAIRS, 48, 128), BF16),
            pltpu.VMEM((64, 128), BF16),
            pltpu.VMEM((4, 16, 128), BF16),
            pltpu.VMEM((4, 16, 128), BF16),
            pltpu.VMEM((GROUP - 1, 16, 128), BF16),
            pltpu.VMEM((GROUP - 1, 16, 128), BF16),
            pltpu.VMEM((96, 256), BF16),
            pltpu.VMEM((LIST * BOXES, 96), BF16),
            pltpu.VMEM((BOXES, 31232), BF16),
            pltpu.VMEM((BOXES, 128), F32),
            sem,
            sem((7,)),
            sem((2,)),
            sem((2,)),
            sem((GROUP - 1,)),
            sem((GROUP - 1,)),
            sem((GROUP - 1,)),
            sem((GROUP - 1,)),
        ],
        compiler_params=pltpu.CompilerParams(
            collective_id=0, has_side_effects=True, vmem_limit_bytes=56 << 20
        ),
    )(
        leaf_offsets,
        latent_charges.reshape(1, ATOMS),
        atom_counts,
        near_boxes,
        far_slots.T,
        branch_slots,
        far_operators,
        factor_tiles(),
    )
    return (near + far).reshape(-1)


def solution(mesh):
    boxes = ("gx", "gy", "gz")
    in_specs = (P(None, boxes), P(boxes), P(boxes), P(None, boxes), P(None, boxes), P(boxes, None, None), P())
    return jax.shard_map(local_part, mesh=mesh, in_specs=in_specs, out_specs=P(boxes), check_vma=False)
```
